128 devices in a mesh: gx: 16 (over z, x), gy: 8 (over y, core).
Axes of the slice: x: 4, y: 4, z: 4, core: 2. Of those that a mesh axis runs over, the one named last changes fastest.
Arguments:
- positions: float32 [3, 32768, 256], P(None, ('gx', 'gy')), may hold values from 0 to 1
- smooth: float32 [32768, 256], P(('gx', 'gy')), may hold values from 0.25 to 0.6
- masses: float32 [32768, 256], P(('gx', 'gy')), may hold values from 0.0002 to 0.002
- entropy: float32 [32768, 256], P(('gx', 'gy')), may hold values from 0.5 to 2
- cell_counts: int32 [32768], P(('gx', 'gy')), may hold values from 64 to 256, as said below
- cell_pairs: int32 [2, 49152], P(None, ('gx', 'gy')), may hold values from 0 to 511, as said below
- pair_count: int32 [128], P(('gx', 'gy')), may hold values from 256 to 384, as said below
- send_cells: int32 [128, 256], P(('gx', 'gy')), may hold values from -1 to 255, as said below
Outputs:
- density: float32 [32768, 256], P(('gx', 'gy'))
- acceleration: float32 [3, 32768, 256], P(None, ('gx', 'gy'))
The draws below stay inside these ranges and needn't reach their ends.
Inputs may be any that keep to these rules, and one draw needn't show every extreme that they name: `cell_counts`: particles of a cell fill the first slots of its tile; some cell is full. `send_cells`: row r, column p * 2 + s: the local cell device r sends to device p in slot s, or -1 for an empty slot. Filled slots of each sender and receiver come first, at least one, with distinct cells; each sender fills all 2 slots for some receiver. `cell_pairs`: on each device the first 256 pairs have a ghost slot (at least 256) as second entry, naming only filled slots, and every filled slot is named; the others name two different local cells. `pair_count`: the live pairs are the first ones of each device; some device has 384.
All inputs are finite; a program needn't handle non-finite values.
Results may differ from the reference program's by a relative error of at most 0.0003.
Values sent between devices are 32-bit elements; how exact they have to be, the bound alone decides.
No kernel may reach another device: no remote copies, remote signals or barrier semaphores. Data moves between devices by JAX's collectives and lax.ppermute only.
A program may use at most 64 MiB of HBM per device.

```python
import math
import jax
import jax.numpy as jnp
from jax import lax

TILE = 256
C_DEV = 256
GHOST_DEV = 256
RANKS = 128
SLOTS = 2
PAIRS_DEV = 384
CELLS = 32768


def shared_sends(key):
    counts = jax.random.randint(jax.random.fold_in(key, 101), (RANKS, RANKS), 1, SLOTS + 1)
    offsets = jax.random.randint(jax.random.fold_in(key, 102), (RANKS,), 1, RANKS)
    row_ids = lax.broadcasted_iota(jnp.int32, (RANKS, RANKS), 0)
    col_ids = lax.broadcasted_iota(jnp.int32, (RANKS, RANKS), 1)
    full_col = (row_ids + offsets[:, None]) % RANKS
    return jnp.where(col_ids == full_col, SLOTS, counts).astype(jnp.int32)


def draw_send_cells(key, part):
    counts = shared_sends(key)
    key = jax.random.fold_in(key, 3)
    scores = jax.random.randint(key, (RANKS, RANKS, C_DEV), 0, 1 << 20) * C_DEV
    scores = scores + lax.broadcasted_iota(jnp.int32, (RANKS, RANKS, C_DEV), 2)
    ranking = jnp.argsort(scores, axis=2)[:, :, :SLOTS].astype(jnp.int32)
    slot_ids = lax.broadcasted_iota(jnp.int32, (RANKS, RANKS, SLOTS), 2)
    chosen = jnp.where(slot_ids < counts[:, :, None], ranking, -1)
    return chosen.reshape(RANKS, RANKS * SLOTS).astype(jnp.int32)


def draw_cell_pairs(key, part):
    counts = shared_sends(key)
    key = jax.random.fold_in(key, 5)
    ghost_ids = lax.broadcasted_iota(jnp.int32, (RANKS, GHOST_DEV), 1)
    source_peer = ghost_ids // SLOTS
    slot_index = ghost_ids % SLOTS
    received = jnp.take_along_axis(counts.T, source_peer, axis=1)
    ghost_code = C_DEV + source_peer * SLOTS + slot_index % received
    scores = jax.random.randint(jax.random.fold_in(key, 1), (RANKS, GHOST_DEV), 0, 1 << 20) * GHOST_DEV + ghost_ids
    ranking = jnp.argsort(scores, axis=1)
    ghost_code = jnp.take_along_axis(ghost_code, ranking, axis=1)
    ghost_first = jax.random.randint(jax.random.fold_in(key, 2), (RANKS, GHOST_DEV), 0, C_DEV)
    local_first = jax.random.randint(jax.random.fold_in(key, 3), (RANKS, PAIRS_DEV - GHOST_DEV), 0, C_DEV)
    offset_step = jax.random.randint(jax.random.fold_in(key, 4), (RANKS, PAIRS_DEV - GHOST_DEV), 1, C_DEV)
    local_second = (local_first + offset_step) % C_DEV
    first_cell = jnp.concatenate([ghost_first, local_first], axis=1).reshape(-1)
    second_cell = jnp.concatenate([ghost_code, local_second], axis=1).reshape(-1)
    return jnp.stack([first_cell, second_cell]).astype(jnp.int32)


def draw_pair_count(key, part):
    key = jax.random.fold_in(key, 7)
    counts = jax.random.randint(key, (RANKS,), GHOST_DEV, PAIRS_DEV + 1)
    chosen = jax.random.randint(jax.random.fold_in(key, 1), (), 0, RANKS)
    return jnp.where(jnp.arange(RANKS, dtype=jnp.int32) == chosen, PAIRS_DEV, counts).astype(jnp.int32)


def draw_cell_counts(key, part):
    key = jax.random.fold_in(key, 9)
    counts = jax.random.randint(key, (CELLS,), TILE // 4, TILE + 1)
    chosen = jax.random.randint(jax.random.fold_in(key, 1), (), 0, CELLS)
    return jnp.where(jnp.arange(CELLS, dtype=jnp.int32) == chosen, TILE, counts).astype(jnp.int32)


def levels(own_key, dims, split, smallest, top_value):
    level, own = 1.0, jax.random.fold_in(own_key, 6)
    for position, blocks in split:
        steps = jnp.exp(jax.random.uniform(jax.random.fold_in(own, position), (blocks,), jnp.float32, smallest / len(split), top_value / len(split)))
        level = level * jnp.repeat(steps, dims[position] // blocks).reshape([-1 if axis == position else 1 for axis in range(len(dims))])
    return level


def setup_inputs(seed: int = 0) -> dict:
    seeds = jax.random.split(jax.random.key(seed), 9)
    return {
        "positions": jnp.clip(1.0 * jax.random.uniform(seeds[0], (3, CELLS, TILE), jnp.float32) ** levels(seeds[0], (3, CELLS, TILE), ((1, 128),), -0.2, 0.2), 0.0, 1.0),
        "smooth": jnp.clip(jnp.exp(math.log(0.6) - 0.8754688 * jax.random.uniform(seeds[1], (CELLS, TILE), jnp.float32) ** levels(seeds[1], (CELLS, TILE), ((0, 128),), -0.2, 0.2)), 0.25, 0.6),
        "masses": jnp.clip(jnp.exp(math.log(0.002) - 2.3025852 * jax.random.uniform(seeds[2], (CELLS, TILE), jnp.float32) ** levels(seeds[2], (CELLS, TILE), ((0, 128),), -0.2, 0.2)), 0.0002, 0.002),
        "entropy": jnp.clip(jnp.exp(math.log(2.0) - 1.3862944 * jax.random.uniform(seeds[3], (CELLS, TILE), jnp.float32) ** levels(seeds[3], (CELLS, TILE), ((0, 128),), -0.2, 0.2)), 0.5, 2.0),
        "cell_counts": draw_cell_counts(jax.random.fold_in(seeds[8], 71), 0),
        "cell_pairs": draw_cell_pairs(jax.random.fold_in(seeds[8], 71), 0),
        "pair_count": draw_pair_count(jax.random.fold_in(seeds[8], 71), 0),
        "send_cells": draw_send_cells(jax.random.fold_in(seeds[8], 71), 0),
    }


KERNEL_NORM = 21.0 / (2.0 * math.pi)

def kernel_weight(distance, smooth_len):
    scaled = distance / smooth_len
    remain = jnp.maximum(1.0 - scaled, 0.0)
    inverse = 1.0 / smooth_len
    return KERNEL_NORM * inverse * inverse * inverse * remain ** 4 * (1.0 + 4.0 * scaled)

def kernel_slope(distance, smooth_len):
    scaled = distance / smooth_len
    remain = jnp.maximum(1.0 - scaled, 0.0)
    inverse = 1.0 / smooth_len
    return -20.0 * KERNEL_NORM * inverse ** 5 * remain ** 3

def separations(near_pos, far_pos):
    offsets = [near_pos[axis_id][:, :, None] - far_pos[axis_id][:, None, :] for axis_id in range(3)]
    distance = jnp.sqrt(offsets[0] * offsets[0] + offsets[1] * offsets[1] + offsets[2] * offsets[2])
    return (offsets, distance)

def density_pair(near_pos, near_smooth, near_mass, far_pos, far_smooth, far_mass):
    offsets, distance = separations(near_pos, far_pos)
    rho_near = lax.optimization_barrier(jnp.sum(kernel_weight(distance, near_smooth[:, :, None]) * far_mass[:, None, :], axis=2))
    rho_far = lax.optimization_barrier(jnp.sum(kernel_weight(distance, far_smooth[:, None, :]) * near_mass[:, :, None], axis=1))
    return (rho_near, rho_far)

def force_pair(near_pos, near_smooth, near_mass, near_factor, far_pos, far_smooth, far_mass, far_factor):
    offsets, distance = separations(near_pos, far_pos)
    coupling = near_factor[:, :, None] * kernel_slope(distance, near_smooth[:, :, None])
    coupling = coupling + far_factor[:, None, :] * kernel_slope(distance, far_smooth[:, None, :])
    near_weighted = coupling * far_mass[:, None, :]
    far_weighted = coupling * near_mass[:, :, None]
    acc_near = jnp.stack([-lax.optimization_barrier(jnp.sum(near_weighted * offsets[axis_id], axis=2)) for axis_id in range(3)])
    acc_far = jnp.stack([lax.optimization_barrier(jnp.sum(far_weighted * offsets[axis_id], axis=1)) for axis_id in range(3)])
    return (acc_near, acc_far)

def reference(positions, smooth, masses, entropy, cell_counts, cell_pairs, pair_count, send_cells):
    group_len = 16
    usable = (lax.broadcasted_iota(jnp.int32, (CELLS, TILE), 1) < cell_counts[:, None]).astype(jnp.float32)
    live_mass = masses * usable
    fields = jnp.concatenate([positions, smooth[None], live_mass[None]], axis=0)
    pair_ids = jnp.arange(RANKS * PAIRS_DEV, dtype=jnp.int32)
    owning = pair_ids // PAIRS_DEV
    living = (pair_ids % PAIRS_DEV < pair_count[owning]).astype(jnp.float32)
    first_cell = owning * C_DEV + cell_pairs[0]
    entry_code = cell_pairs[1]
    ghost_slot = jnp.maximum(entry_code - C_DEV, 0)
    source_peer = ghost_slot // SLOTS
    column = owning * SLOTS + ghost_slot % SLOTS
    remote_cell = source_peer * C_DEV + send_cells[source_peer, column]
    second_cell = jnp.where(entry_code < C_DEV, owning * C_DEV + entry_code, remote_cell).astype(jnp.int32)
    turns = RANKS * PAIRS_DEV // group_len
    pair_items = (first_cell.reshape(turns, group_len), second_cell.reshape(turns, group_len), living.reshape(turns, group_len))
    group_ids = jnp.arange(CELLS // group_len, dtype=jnp.int32)

    def self_density(group_index):
        piece = lax.dynamic_slice_in_dim(fields, group_index * group_len, group_len, 1)
        return density_pair(piece[0:3], piece[3], piece[4], piece[0:3], piece[3], piece[4])[0]

    def density_step(running, entry_item):
        first_ids, second_ids, alive_now = entry_item
        near_side = jnp.take(fields, first_ids, axis=1)
        far_side = jnp.take(fields, second_ids, axis=1)
        rho_near, rho_far = density_pair(near_side[0:3], near_side[3], near_side[4] * alive_now[:, None], far_side[0:3], far_side[3], far_side[4] * alive_now[:, None])
        return (running.at[first_ids].add(rho_near).at[second_ids].add(rho_far), None)
    self_rho = lax.map(self_density, group_ids).reshape(CELLS, TILE)
    pair_rho, _ = lax.scan(density_step, jnp.zeros((CELLS, TILE), jnp.float32), pair_items)
    density = (self_rho + pair_rho) * usable
    clipped_rho = jnp.where(usable > 0, density, 1.0)
    factor = jnp.where(usable > 0, entropy * clipped_rho ** (-1.0 / 3.0), 0.0)

    def self_force(group_index):
        piece = lax.dynamic_slice_in_dim(fields, group_index * group_len, group_len, 1)
        piece_factor = lax.dynamic_slice_in_dim(factor, group_index * group_len, group_len, 0)
        return force_pair(piece[0:3], piece[3], piece[4], piece_factor, piece[0:3], piece[3], piece[4], piece_factor)[0]

    def force_step(running, entry_item):
        first_ids, second_ids, alive_now = entry_item
        near_side = jnp.take(fields, first_ids, axis=1)
        far_side = jnp.take(fields, second_ids, axis=1)
        acc_near, acc_far = force_pair(near_side[0:3], near_side[3], near_side[4] * alive_now[:, None], jnp.take(factor, first_ids, axis=0), far_side[0:3], far_side[3], far_side[4] * alive_now[:, None], jnp.take(factor, second_ids, axis=0))
        return (running.at[:, first_ids].add(acc_near).at[:, second_ids].add(acc_far), None)
    self_acc = jnp.moveaxis(lax.map(self_force, group_ids), 1, 0).reshape(3, CELLS, TILE)
    pair_acc, _ = lax.scan(force_step, jnp.zeros((3, CELLS, TILE), jnp.float32), pair_items)
    acceleration = (self_acc + pair_acc) * usable[None]
    return (density, acceleration)
```

```python
import functools
import math

import jax
import jax.numpy as jnp
from jax import lax
from jax.experimental import pallas as pl
from jax.experimental.pallas import tpu as pltpu
from jax.sharding import PartitionSpec as P

KERNEL_NORM = 21.0 / (2.0 * math.pi)
AXES = ("gx", "gy")
LANES = 128
TILE = 256
ROWS = 64
CHUNKS = TILE // ROWS
TINY = 1e-30
F32 = jnp.float32
BF16 = jnp.bfloat16

ROW_NORM, ROW_ONE, ROW_H, ROW_MASS, ROW_G = 3, 4, 5, 6, 7

NN = (((1,), (0,)), ((), ()))
TN = (((0,), (0,)), ((), ()))
NT = (((1,), (1,)), ((), ()))


def mxu(a, b, dims):
    return lax.dot_general(a, b, dims, preferred_element_type=F32)


def pieces3(x):
    a = x.astype(BF16).astype(F32)
    r = x - a
    b = r.astype(BF16).astype(F32)
    c = r - b
    return a, b, c


def left_stack(x):
    a, b, c = pieces3(x)
    return jnp.concatenate([a, a, b, b, a, c], axis=0).astype(BF16)


def right_stack(x):
    a, b, c = pieces3(x)
    return jnp.concatenate([a, b, a, b, c, a], axis=0).astype(BF16)


def hi_lo_rows(x):
    hi = x.astype(BF16).astype(F32)
    return jnp.concatenate([hi, x - hi], axis=0).astype(BF16)


def twice(x):
    return jnp.concatenate([x, x], axis=1)


def row_fields(f_ref, i):
    block = f_ref[i >> 1]
    return pltpu.roll(block, (i & 1) * ROWS, axis=1)[:, :ROWS]


def lane_fields(f_ref, j):
    return jnp.concatenate([f_ref[2 * j], f_ref[2 * j + 1]], axis=1)


def distances(f_ref, pick, i, j):
    left = left_stack(row_fields(f_ref, i))
    lanes = lane_fields(f_ref, j)
    row = lax.broadcasted_iota(jnp.int32, (8, TILE), 0)
    norm = lanes[ROW_NORM : ROW_NORM + 1, :]
    right = jnp.where(row < 3, -2.0 * lanes, jnp.where(row == ROW_ONE, norm, jnp.where(row == ROW_NORM, 1.0, 0.0)))
    return mxu(left, right_stack(right), TN), mxu(left, pick, TN)


def lane_row(f_ref, j, which):
    return jnp.concatenate(
        [f_ref[2 * j, which : which + 1, :], f_ref[2 * j + 1, which : which + 1, :]], axis=1
    )


def fold_rows(x):
    total = x[0:8]
    for k in range(1, x.shape[0] // 8):
        total = total + x[8 * k : 8 * k + 8]
    return total


def density_self_values(parts, f_ref, i, j):
    squared, column = parts
    squared = jnp.maximum(squared, TINY)
    dist = squared * lax.rsqrt(squared)
    h = lane_row(f_ref, j, ROW_H)
    t = jnp.maximum(h - dist, 0.0)
    t = t * t
    return fold_rows(t * t * (h + 4.0 * dist) * twice(column))


def density_pair_values(parts, f_ref, i, j):
    squared, column = parts
    squared = jnp.maximum(squared, TINY)
    dist = squared * lax.rsqrt(squared)
    four = 4.0 * dist
    h_row, m_row = twice(column[:, :LANES]), twice(column[:, LANES:])
    h, m = lane_row(f_ref, j, ROW_H), lane_row(f_ref, j, ROW_MASS)
    t = jnp.maximum(h_row - dist, 0.0)
    t = t * t
    near = t * t * (h_row + four) * m
    s = jnp.maximum(h - dist, 0.0)
    s = s * s
    far = s * s * (h + four) * m_row
    return near[:, :LANES] + near[:, LANES:], fold_rows(far)


def density_self_store(values, f_ref, out, i, j):
    out[2 * j] += values[:, :LANES]
    out[2 * j + 1] += values[:, LANES:]


def density_pair_store(values, f_ref, out, col, i, j):
    near, far = values
    out[2 * j] += far[:, :LANES]
    out[2 * j + 1] += far[:, LANES:]
    lane = lax.broadcasted_iota(jnp.int32, (ROWS, LANES), 1)
    total = jnp.sum(near, axis=1, keepdims=True)
    col[i >> 7] += jnp.where(lane == (i & 127), total, 0.0)


def force_values(parts, f_ref, i, j):
    squared, column = parts
    squared = jnp.maximum(squared, TINY)
    dist = squared * lax.rsqrt(squared)
    h_row, g_row = twice(column[:, :LANES]), twice(column[:, LANES:])
    h, g = lane_row(f_ref, j, ROW_H), lane_row(f_ref, j, ROW_G)
    a = jnp.maximum(h_row - dist, 0.0)
    b = jnp.maximum(h - dist, 0.0)
    coupling = g_row * (a * a * a) + g * (b * b * b)
    hi = coupling.astype(BF16)
    lo = (coupling - hi.astype(F32)).astype(BF16)
    return hi, lo


def force_far_store(values, f_ref, out, i, j):
    hi, lo = values
    rows = row_fields(f_ref, i)
    moments = hi_lo_rows(rows * rows[ROW_MASS : ROW_MASS + 1, :])
    far = fold_rows(mxu(moments, hi, NN) + mxu(moments, lo, NN))
    out[2 * j] += far[:, :LANES]
    out[2 * j + 1] += far[:, LANES:]


def force_pair_store(values, f_ref, out, i, j):
    hi, lo = values
    force_far_store(values, f_ref, out, i, j)
    lanes = lane_fields(f_ref, j)
    moments = hi_lo_rows(lanes * lanes[ROW_MASS : ROW_MASS + 1, :])
    near = twice(fold_rows(mxu(moments, hi, NT) + mxu(moments, lo, NT)))
    lane = lax.broadcasted_iota(jnp.int32, (8, LANES), 1)
    out[i >> 1] += jnp.where((lane >> 6) == (i & 1), near, 0.0)


def sweep(unroll, lead, lag, count, units, stage_a, stage_b, stage_c):
    def body(step, carry):
        ids = []
        for k in range(unroll):
            code = units[step * unroll + k]
            ids.append((code >> 16, code & 0xFFFF))
        parts, values = {}, {}
        for k in range(-lead, unroll + lag):
            if 0 <= k + lead < unroll:
                parts[k + lead] = stage_a(*ids[k + lead])
            if 0 <= k < unroll:
                values[k] = stage_b(parts.pop(k), *ids[k])
            if 0 <= k - lag < unroll:
                stage_c(values.pop(k - lag), *ids[k - lag])
        return carry

    lax.fori_loop(0, count, body, 0)


def density_self_kernel(unroll, count, units, f_ref, pick, out):
    out[...] = jnp.zeros_like(out)
    sweep(
        unroll, 2, 1, count[0], units,
        lambda i, j: distances(f_ref, pick[:, LANES:], i, j),
        lambda p, i, j: density_self_values(p, f_ref, i, j),
        lambda v, i, j: density_self_store(v, f_ref, out, i, j),
    )


def density_pair_kernel(unroll, count, units, f_ref, pick, out, col):
    out[...] = jnp.zeros_like(out)
    col[...] = jnp.zeros_like(col)
    sweep(
        unroll, 3, 2, count[0], units,
        lambda i, j: distances(f_ref, pick[...], i, j),
        lambda p, i, j: density_pair_values(p, f_ref, i, j),
        lambda v, i, j: density_pair_store(v, f_ref, out, col, i, j),
    )


def force_kernel(unroll, both, count, units, f_ref, pick, out):
    out[...] = jnp.zeros_like(out)
    store = force_pair_store if both else force_far_store
    sweep(
        unroll, 3, 3, count[0], units,
        lambda i, j: distances(f_ref, pick[...], i, j),
        lambda p, i, j: force_values(p, f_ref, i, j),
        lambda v, i, j: store(v, f_ref, out, i, j),
    )


def run_kernel(body, name, count, units, fields, pick, with_col, est_units):
    smem = pl.BlockSpec(memory_space=pltpu.SMEM)
    vmem = pl.BlockSpec(memory_space=pltpu.VMEM)
    blocks = fields.shape[0]
    shapes = [jax.ShapeDtypeStruct((blocks, 8, LANES), F32)]
    if with_col:
        groups = (2 * blocks + LANES - 1) // LANES
        shapes.append(jax.ShapeDtypeStruct((groups, ROWS, LANES), F32))
    out = pl.pallas_call(
        body,
        out_shape=shapes,
        in_specs=[smem, smem, vmem, vmem],
        out_specs=[vmem] * len(shapes),
        name=name,
        compiler_params=pltpu.CompilerParams(vmem_limit_bytes=40 * 1024 * 1024),
        cost_estimate=pl.CostEstimate(
            flops=est_units * ROWS * TILE * 2000, bytes_accessed=2 * fields.size * 4, transcendentals=0
        ),
    )(count, units, fields, pick)
    return out


def pick_matrix(second):
    k = lax.broadcasted_iota(jnp.int32, (48, TILE), 0)
    lane = lax.broadcasted_iota(jnp.int32, (48, TILE), 1)
    group, row = k // 8, k % 8
    used = (group == 0) | (group == 2) | (group == 5)
    return (used & (row == jnp.where(lane < LANES, ROW_H, second))).astype(BF16)


def compact(valid, code, spare, unroll):
    num = valid.shape[0]
    flags = valid.astype(jnp.int32)
    ids = jnp.arange(num, dtype=jnp.int32)
    rank = jnp.sum(jnp.where(ids[None, :] < ids[:, None], flags[None, :], 0), axis=1)
    total = jnp.sum(flags)
    hit = (rank[None, :] == ids[:, None]) & valid[None, :]
    listed = jnp.sum(jnp.where(hit, code[None, :], 0), axis=1)
    listed = jnp.where(ids < total, listed, spare)
    return listed.astype(jnp.int32), ((total + unroll - 1) // unroll).reshape(1).astype(jnp.int32)


def look_up(table, ids):
    slots = jnp.arange(table.shape[0], dtype=jnp.int32)
    return jnp.sum(jnp.where(ids[:, None] == slots[None, :], table[None, :], 0), axis=1)


def pair_units(first, second, live, counts, unroll):
    num_cells = counts.shape[0]
    n_first, n_second = look_up(counts, first), look_up(counts, second)
    swap = n_second < n_first
    rows = jnp.where(swap, second, first)
    lanes = jnp.where(swap, first, second)
    chunks = (jnp.minimum(n_first, n_second) + ROWS - 1) // ROWS
    step = jnp.arange(CHUNKS, dtype=jnp.int32)
    valid = (step[None, :] < chunks[:, None]) & live[:, None]
    code = ((rows[:, None] * CHUNKS + step[None, :]) << 16) | lanes[:, None]
    spare = ((num_cells * CHUNKS) << 16) | num_cells
    return compact(valid.reshape(-1), code.reshape(-1), spare, unroll)


def to_blocks(fields):
    cells = fields.shape[0]
    blocks = fields.reshape(cells, 8, 2, LANES).transpose(0, 2, 1, 3).reshape(2 * cells, 8, LANES)
    return jnp.concatenate([blocks, jnp.zeros((2, 8, LANES), F32)], axis=0)


def spread(x):
    c = x[0:3] - 0.5
    norm = c[0] * c[0] + c[1] * c[1] + c[2] * c[2]
    return jnp.stack([c[0], c[1], c[2], norm, jnp.ones_like(norm), x[3], x[4], jnp.zeros_like(norm)], axis=1)


def with_factor(fields, g):
    return jnp.concatenate([fields[:, :7], g[:, None, :]], axis=1)


def from_blocks(blocks, cells):
    return blocks[: 2 * cells].reshape(cells, 2, 8, LANES).transpose(2, 0, 1, 3).reshape(8, cells, TILE)


def from_columns(col, cells):
    return col.transpose(0, 2, 1).reshape(-1, TILE)[:cells]


def trade(payload):
    return lax.all_to_all(payload, AXES, split_axis=1, concat_axis=1, tiled=True)


def local(positions, smooth, masses, entropy, cell_counts, cell_pairs, pair_count, send_cells):
    cells, tile = smooth.shape
    num_pairs = cell_pairs.shape[1]
    unroll = 16
    usable = (lax.broadcasted_iota(jnp.int32, (cells, tile), 1) < cell_counts[:, None]).astype(F32)
    live_mass = masses * usable
    targets = send_cells[0]
    clipped = jnp.maximum(targets, 0)
    local_raw = jnp.concatenate([positions, smooth[None], live_mass[None]], axis=0)
    ghosts_raw = trade(jnp.take(local_raw, clipped, axis=1))
    slots = ghosts_raw.shape[1]

    own = spread(local_raw)
    own_blocks = to_blocks(own)
    pick_m, pick_g = pick_matrix(ROW_MASS), pick_matrix(ROW_G)

    step = jnp.arange(CHUNKS, dtype=jnp.int32)
    ids = jnp.arange(cells, dtype=jnp.int32)
    self_valid = step[None, :] < ((cell_counts + ROWS - 1) // ROWS)[:, None]
    self_code = ((ids[:, None] * CHUNKS + step[None, :]) << 16) | ids[:, None]
    self_units, self_count = compact(
        self_valid.reshape(-1), self_code.reshape(-1), ((cells * CHUNKS) << 16) | cells, unroll
    )
    live_pair = jnp.arange(num_pairs, dtype=jnp.int32) < pair_count[0]
    first, second = cell_pairs[0], cell_pairs[1]
    inner_units, inner_count = pair_units(first[slots:], second[slots:], live_pair[slots:], cell_counts, unroll)

    (self_rho,) = run_kernel(
        functools.partial(density_self_kernel, unroll), "density_self", self_count, self_units, own_blocks, pick_m, False, 768
    )

    ghost_counts = jnp.sum((ghosts_raw[4] > 0).astype(jnp.int32), axis=1)
    all_counts = jnp.concatenate([cell_counts, ghost_counts])
    outer_units, outer_count = pair_units(first[:slots], second[:slots], live_pair[:slots], all_counts, unroll)
    ghosts = spread(ghosts_raw)
    everything = jnp.concatenate([own, ghosts], axis=0)
    all_blocks = to_blocks(everything)

    outer_rho, outer_col = run_kernel(
        functools.partial(density_pair_kernel, unroll), "density_outer", outer_count, outer_units, all_blocks, pick_m, True, 640
    )
    outer_total = jnp.sum(from_blocks(outer_rho, cells + slots), axis=0) + from_columns(outer_col, cells + slots)
    scale = KERNEL_NORM / everything[:, ROW_H] ** 8
    outer_total = outer_total * scale
    returned_rho = trade(outer_total[None, cells:])[0]

    inner_rho, inner_col = run_kernel(
        functools.partial(density_pair_kernel, unroll), "density_inner", inner_count, inner_units, own_blocks, pick_m, True, 320
    )
    inner_total = jnp.sum(from_blocks(self_rho + inner_rho, cells), axis=0) + from_columns(inner_col, cells)
    selector = (targets[None, :] == lax.broadcasted_iota(jnp.int32, (cells, slots), 0)).astype(F32)
    credited = jnp.dot(selector, returned_rho, precision=lax.Precision.HIGHEST, preferred_element_type=F32)
    density = (inner_total * scale[:cells] + outer_total[:cells] + credited) * usable
    clipped_rho = jnp.where(usable > 0, density, 1.0)
    factor = jnp.where(usable > 0, entropy * clipped_rho ** (-1.0 / 3.0), 0.0)

    ghost_factor = trade(jnp.take(factor, clipped, axis=0)[None])[0]

    own_g = 20.0 * scale[:cells] * factor
    own_blocks_g = to_blocks(with_factor(own, own_g))
    (self_acc,) = run_kernel(
        functools.partial(force_kernel, unroll, False), "force_self", self_count, self_units, own_blocks_g, pick_g, False, 768
    )
    ghost_g = 20.0 * scale[cells:] * ghost_factor
    all_blocks_g = to_blocks(with_factor(everything, jnp.concatenate([own_g, ghost_g], axis=0)))
    (outer_acc,) = run_kernel(
        functools.partial(force_kernel, unroll, True), "force_outer", outer_count, outer_units, all_blocks_g, pick_g, False, 640
    )
    outer_acc = from_blocks(outer_acc, cells + slots)
    ghost_acc = ghosts[:, 0:3].transpose(1, 0, 2) * outer_acc[ROW_ONE, cells:] - outer_acc[0:3, cells:]
    returned_acc = trade(ghost_acc)

    (inner_acc,) = run_kernel(
        functools.partial(force_kernel, unroll, True), "force_inner", inner_count, inner_units, own_blocks_g, pick_g, False, 320
    )
    moments = from_blocks(self_acc + inner_acc, cells) + outer_acc[:, :cells]
    credited_acc = jnp.einsum(
        "cg,kgp->kcp", selector, returned_acc, precision=lax.Precision.HIGHEST, preferred_element_type=F32
    )
    own_acc = own[:, 0:3].transpose(1, 0, 2) * moments[ROW_ONE] - moments[0:3]
    acceleration = (own_acc + credited_acc) * usable[None]
    return (density, acceleration)


def solution(mesh):
    in_specs = (
        P(None, AXES, None),
        P(AXES, None),
        P(AXES, None),
        P(AXES, None),
        P(AXES),
        P(None, AXES),
        P(AXES),
        P(AXES, None),
    )
    out_specs = (P(AXES, None), P(None, AXES, None))
    return jax.shard_map(local, mesh=mesh, in_specs=in_specs, out_specs=out_specs, check_vma=False)
```

```python
import functools
import math

import jax
import jax.numpy as jnp
from jax import lax
from jax.experimental import pallas as pl
from jax.experimental.pallas import tpu as pltpu
from jax.sharding import PartitionSpec as P

KERNEL_NORM = 21.0 / (2.0 * math.pi)
AXES = ("gx", "gy")
LANES = 128
TILE = 256
ROWS = 64
CHUNKS = TILE // ROWS
TINY = 1e-30
F32 = jnp.float32
BF16 = jnp.bfloat16

ROW_NORM, ROW_ONE, ROW_H, ROW_MASS, ROW_G = 3, 4, 5, 6, 7

NN = (((1,), (0,)), ((), ()))
TN = (((0,), (0,)), ((), ()))
NT = (((1,), (1,)), ((), ()))


def mxu(a, b, dims):
    return lax.dot_general(a, b, dims, preferred_element_type=F32)


def pieces3(x):
    a = x.astype(BF16).astype(F32)
    r = x - a
    b = r.astype(BF16).astype(F32)
    c = r - b
    return a, b, c


def left_stack(x):
    a, b, c = pieces3(x)
    return jnp.concatenate([a, a, b, b, a, c], axis=0).astype(BF16)


def right_stack(x):
    a, b, c = pieces3(x)
    return jnp.concatenate([a, b, a, b, c, a], axis=0).astype(BF16)


def hi_lo_rows(x):
    hi = x.astype(BF16).astype(F32)
    return jnp.concatenate([hi, x - hi], axis=0).astype(BF16)


def twice(x):
    return jnp.concatenate([x, x], axis=1)


def row_fields(f_ref, i):
    block = f_ref[i >> 2, (i >> 1) & 1]
    return pltpu.roll(block, (i & 1) * ROWS, axis=1)[:, :ROWS]


def lane_fields(f_ref, j):
    return jnp.concatenate([f_ref[j, 0], f_ref[j, 1]], axis=1)


def distances(f_ref, pick, i, j):
    left = left_stack(row_fields(f_ref, i))
    lanes = lane_fields(f_ref, j)
    row = lax.broadcasted_iota(jnp.int32, (8, TILE), 0)
    norm = lanes[ROW_NORM : ROW_NORM + 1, :]
    right = jnp.where(row < 3, -2.0 * lanes, jnp.where(row == ROW_ONE, norm, jnp.where(row == ROW_NORM, 1.0, 0.0)))
    return mxu(left, right_stack(right), TN), mxu(left, pick, TN)


def lane_row(f_ref, j, which):
    return jnp.concatenate([f_ref[j, 0, which : which + 1, :], f_ref[j, 1, which : which + 1, :]], axis=1)


def fold_rows(x):
    total = x[0:8]
    for k in range(1, x.shape[0] // 8):
        total = total + x[8 * k : 8 * k + 8]
    return total


def add_lanes(out, j, values):
    out[j, 0] += values[:, :LANES]
    out[j, 1] += values[:, LANES:]


def add_rows(out, i, values):
    lane = lax.broadcasted_iota(jnp.int32, (8, LANES), 1)
    out[i >> 2, (i >> 1) & 1] += jnp.where((lane >> 6) == (i & 1), twice(values), 0.0)


def root(squared):
    squared = jnp.maximum(squared, TINY)
    return squared * lax.rsqrt(squared)


def density_self_values(parts, f_ref, i, j):
    squared, column = parts
    dist = root(squared)
    h = lane_row(f_ref, j, ROW_H)
    t = jnp.maximum(h - dist, 0.0)
    t = t * t
    return fold_rows(t * t * (h + 4.0 * dist) * twice(column))


def density_pair_values(parts, f_ref, i, j):
    squared, column = parts
    dist = root(squared)
    four = 4.0 * dist
    h_row, m_row = twice(column[:, :LANES]), twice(column[:, LANES:])
    h, m = lane_row(f_ref, j, ROW_H), lane_row(f_ref, j, ROW_MASS)
    t = jnp.maximum(h_row - dist, 0.0)
    t = t * t
    near = t * t * (h_row + four) * m
    s = jnp.maximum(h - dist, 0.0)
    s = s * s
    far = s * s * (h + four) * m_row
    return hi_lo(near[:, :LANES] + near[:, LANES:]), fold_rows(far)


def density_pair_store(values, out, i, j):
    (hi, lo), far = values
    add_lanes(out, j, far)
    one = (lax.broadcasted_iota(jnp.int32, (16, LANES), 0) == 0).astype(BF16)
    add_rows(out, i, (mxu(one, hi, NT) + mxu(one, lo, NT))[0:8])


def hi_lo(x):
    hi = x.astype(BF16)
    return hi, (x - hi.astype(F32)).astype(BF16)


def force_values(parts, f_ref, i, j):
    squared, column = parts
    dist = root(squared)
    h_row, g_row = twice(column[:, :LANES]), twice(column[:, LANES:])
    h, g = lane_row(f_ref, j, ROW_H), lane_row(f_ref, j, ROW_G)
    a = jnp.maximum(h_row - dist, 0.0)
    b = jnp.maximum(h - dist, 0.0)
    return hi_lo(g_row * (a * a * a) + g * (b * b * b))


def moments(x):
    return hi_lo_rows(x * x[ROW_MASS : ROW_MASS + 1, :])


def force_store(both, values, f_ref, out, i, j):
    hi, lo = values
    rows = moments(row_fields(f_ref, i))
    add_lanes(out, j, fold_rows(mxu(rows, hi, NN) + mxu(rows, lo, NN)))
    if both:
        lanes = moments(lane_fields(f_ref, j))
        add_rows(out, i, fold_rows(mxu(lanes, hi, NT) + mxu(lanes, lo, NT)))


def sweep(unroll, lead, lag, count, units, stage_a, stage_b, stage_c):
    def body(step, carry):
        ids = []
        for k in range(unroll):
            code = units[step * unroll + k]
            ids.append((code >> 16, code & 0xFFFF))
        parts, values = {}, {}
        for k in range(-lead, unroll + lag):
            if 0 <= k + lead < unroll:
                parts[k + lead] = stage_a(*ids[k + lead])
            if 0 <= k < unroll:
                values[k] = stage_b(parts.pop(k), *ids[k])
            if 0 <= k - lag < unroll:
                stage_c(values.pop(k - lag), *ids[k - lag])
        return carry

    lax.fori_loop(0, count, body, 0)


def sweep_density(unroll, both, count, units, f_ref, pick, out):
    out[...] = jnp.zeros_like(out)
    if both:
        sweep(
            unroll, 2, 2, count[0], units,
            lambda i, j: distances(f_ref, pick[...], i, j),
            lambda p, i, j: density_pair_values(p, f_ref, i, j),
            lambda v, i, j: density_pair_store(v, out, i, j),
        )
    else:
        sweep(
            unroll, 2, 1, count[0], units,
            lambda i, j: distances(f_ref, pick[:, LANES:], i, j),
            lambda p, i, j: density_self_values(p, f_ref, i, j),
            lambda v, i, j: add_lanes(out, j, v),
        )


def sweep_force(unroll, both, count, units, f_ref, pick, out):
    out[...] = jnp.zeros_like(out)
    sweep(
        unroll, 2, 2, count[0], units,
        lambda i, j: distances(f_ref, pick[...], i, j),
        lambda p, i, j: force_values(p, f_ref, i, j),
        lambda v, i, j: force_store(both, v, f_ref, out, i, j),
    )


def density_scale(h):
    h2 = h * h
    h4 = h2 * h2
    return KERNEL_NORM / (h4 * h4)


def each_group(cells, body):
    def step(k, carry):
        for half in range(2):
            body(pl.multiple_of(k * 8, 8), half)
        return carry

    lax.fori_loop(0, cells // 8, step, 0)


def half_lanes(half):
    return slice(half * LANES, (half + 1) * LANES)


def prepare_kernel(counts, targets, pos, smooth, masses, fields, outgoing):
    cells = smooth.shape[0]
    fields[cells] = jnp.zeros((2, 8, LANES), F32)
    sub = lax.broadcasted_iota(jnp.int32, (8, LANES), 0)
    lane = lax.broadcasted_iota(jnp.int32, (8, LANES), 1)

    def group(c, half):
        count = jnp.zeros((8, LANES), jnp.int32)
        for k in range(8):
            count = jnp.where(sub == k, counts[c + k], count)
        at = (pl.ds(c, 8), half_lanes(half))
        x, y, z = (pos[k, at[0], at[1]] - 0.5 for k in range(3))
        mass = jnp.where(lane + half * LANES < count, masses[at], 0.0)
        rows = (x, y, z, x * x + y * y + z * z, jnp.ones_like(x), smooth[at], mass, count.astype(F32))
        for k in range(8):
            fields[pl.ds(c, 8), half, k, :] = rows[k]

    each_group(cells, group)

    def export(k, carry):
        for s in range(8):
            slot = k * 8 + s
            outgoing[slot] = fields[jnp.maximum(targets[slot], 0)]
        return carry

    lax.fori_loop(0, outgoing.shape[0] // 8, export, 0)


def density_inner_kernel(unroll, both, count, units, f_ref, pick, out):
    sweep_density(unroll, both, count, units, f_ref, pick, out)


def load_all(own, ghosts, everything, sems):
    first = own.shape[0]
    copies = [
        pltpu.make_async_copy(own, everything.at[pl.ds(0, first)], sems.at[0]),
        pltpu.make_async_copy(ghosts, everything.at[pl.ds(first, ghosts.shape[0])], sems.at[1]),
    ]
    for copy in copies:
        copy.start()
    for copy in copies:
        copy.wait()


def density_outer_kernel(unroll, count, units, own, ghosts, pick, own_out, ghost_out, everything, acc, sems):
    load_all(own, ghosts, everything, sems)
    sweep_density(unroll, True, count, units, everything, pick, acc)
    first = own.shape[0]

    def finish_own(c, half):
        own_out[pl.ds(c, 8), half_lanes(half)] = jnp.sum(acc[pl.ds(c, 8), half], axis=1)

    def finish_ghost(c, half):
        total = jnp.sum(acc[pl.ds(first + c, 8), half], axis=1)
        scale = density_scale(everything[pl.ds(first + c, 8), half, ROW_H, :])
        ghost_out[pl.ds(c, 8), 0, half_lanes(half)] = total * scale

    each_group(own_out.shape[0], finish_own)
    each_group(ghost_out.shape[0], finish_ghost)


def factor_kernel(targets, self_acc, inner_acc, outer, returned, fields, entropy, density, fields_g, outgoing, total, scaled, g_all):
    cells = density.shape[0]
    fields_g[...] = fields[...]

    def gather(c, half):
        at = (pl.ds(c, 8), half_lanes(half))
        both = jnp.sum(self_acc[pl.ds(c, 8), half] + inner_acc[pl.ds(c, 8), half], axis=1) + outer[at]
        scale = density_scale(fields[pl.ds(c, 8), half, ROW_H, :])
        total[at] = both * scale
        scaled[at] = 20.0 * scale

    each_group(cells, gather)

    def credit(k, carry):
        for s in range(8):
            slot = k * 8 + s
            target = targets[slot]
            at = pl.ds(jnp.where(target < 0, cells, target), 1)
            total[at, :] += returned[slot]
        return carry

    lax.fori_loop(0, returned.shape[0] // 8, credit, 0)

    def finish(c, half):
        at = (pl.ds(c, 8), half_lanes(half))
        live = fields[pl.ds(c, 8), half, ROW_MASS, :] > 0.0
        rho = jnp.where(live, total[at], 0.0)
        density[at] = rho
        safe = jnp.where(live, rho, 1.0)
        g = jnp.where(live, entropy[at] * jnp.exp(jnp.log(safe) * (-1.0 / 3.0)) * scaled[at], 0.0)
        g_all[at] = g
        fields_g[pl.ds(c, 8), half, ROW_G, :] = g

    each_group(cells, finish)

    def export(k, carry):
        for s in range(8):
            slot = k * 8 + s
            outgoing[slot] = g_all[pl.ds(jnp.maximum(targets[slot], 0), 1), :]
        return carry

    lax.fori_loop(0, outgoing.shape[0] // 8, export, 0)


def accelerate(f_ref, sums, c, half):
    f, s = f_ref[c, half], sums[c, half]
    return f * s[ROW_ONE : ROW_ONE + 1, :] - s


def force_inner_kernel(unroll, both, count, units, f_ref, pick, out):
    sweep_force(unroll, both, count, units, f_ref, pick, out)

    def finish(k, carry):
        for s in range(4):
            for half in range(2):
                out[4 * k + s, half] = accelerate(f_ref, out, 4 * k + s, half)
        return carry

    lax.fori_loop(0, out.shape[0] // 4, finish, 0)


def force_outer_kernel(unroll, count, units, own, ghosts, ghost_g, pick, own_out, ghost_out, everything, acc, sems):
    load_all(own, ghosts, everything, sems)
    first = own.shape[0]

    def insert(c, half):
        everything[pl.ds(first + c, 8), half, ROW_G, :] = ghost_g[pl.ds(c, 8), 0, half_lanes(half)]

    each_group(ghost_g.shape[0], insert)
    sweep_force(unroll, True, count, units, everything, pick, acc)

    def finish(k, carry):
        for s in range(4):
            for half in range(2):
                own_out[4 * k + s, half] = accelerate(everything, acc, 4 * k + s, half)
                ghost_out[4 * k + s, half] = accelerate(everything, acc, first + 4 * k + s, half)[0:4]
        return carry

    lax.fori_loop(0, own_out.shape[0] // 4, finish, 0)


def final_kernel(targets, self_acc, inner_acc, outer_acc, returned, fields, acceleration, total):
    cells = outer_acc.shape[0]

    def gather(k, carry):
        for s in range(4):
            c = 4 * k + s
            total[c] = self_acc[c] + inner_acc[c] + outer_acc[c]
        return carry

    lax.fori_loop(0, cells // 4, gather, 0)

    def credit(k, carry):
        for s in range(8):
            slot = k * 8 + s
            target = targets[slot]
            at = jnp.where(target < 0, cells, target)
            for half in range(2):
                total[at, half, 0:4, :] += returned[slot, half]
        return carry

    lax.fori_loop(0, returned.shape[0] // 8, credit, 0)

    def finish(c, half):
        live = fields[pl.ds(c, 8), half, ROW_MASS, :] > 0.0
        for k in range(3):
            acceleration[k, pl.ds(c, 8), half_lanes(half)] = jnp.where(live, total[pl.ds(c, 8), half, k, :], 0.0)

    each_group(cells, finish)


SMEM = pl.BlockSpec(memory_space=pltpu.SMEM)
VMEM = pl.BlockSpec(memory_space=pltpu.VMEM)
ANY = pl.BlockSpec(memory_space=pl.ANY)


def launch(body, name, in_specs, shapes, args, scratch=(), flops=0, limit=40):
    return pl.pallas_call(
        body,
        out_shape=[jax.ShapeDtypeStruct(shape, F32) for shape in shapes],
        in_specs=in_specs,
        out_specs=[VMEM] * len(shapes),
        scratch_shapes=list(scratch),
        name=name,
        compiler_params=pltpu.CompilerParams(vmem_limit_bytes=limit * 1024 * 1024),
        cost_estimate=pl.CostEstimate(flops=flops, bytes_accessed=1 << 21, transcendentals=0),
    )(*args)


def pick_matrix(second):
    k = lax.broadcasted_iota(jnp.int32, (48, TILE), 0)
    lane = lax.broadcasted_iota(jnp.int32, (48, TILE), 1)
    group, row = k // 8, k % 8
    used = (group == 0) | (group == 2) | (group == 5)
    return (used & (row == jnp.where(lane < LANES, ROW_H, second))).astype(BF16)


def compact(valid, code, spare, unroll):
    num = valid.shape[0]
    flags = valid.astype(jnp.int32)
    ids = jnp.arange(num, dtype=jnp.int32)
    rank = jnp.sum(jnp.where(ids[None, :] < ids[:, None], flags[None, :], 0), axis=1)
    total = jnp.sum(flags)
    hit = (rank[None, :] == ids[:, None]) & valid[None, :]
    listed = jnp.sum(jnp.where(hit, code[None, :], 0), axis=1)
    listed = jnp.where(ids < total, listed, spare)
    return listed.astype(jnp.int32), ((total + unroll - 1) // unroll).reshape(1).astype(jnp.int32)


def look_up(table, ids):
    slots = jnp.arange(table.shape[0], dtype=jnp.int32)
    return jnp.sum(jnp.where(ids[:, None] == slots[None, :], table[None, :], 0), axis=1)


def pair_units(first, second, live, counts, spare, unroll):
    n_first, n_second = look_up(counts, first), look_up(counts, second)
    swap = n_second < n_first
    rows = jnp.where(swap, second, first)
    lanes = jnp.where(swap, first, second)
    chunks = (jnp.minimum(n_first, n_second) + ROWS - 1) // ROWS
    step = jnp.arange(CHUNKS, dtype=jnp.int32)
    valid = (step[None, :] < chunks[:, None]) & live[:, None]
    code = ((rows[:, None] * CHUNKS + step[None, :]) << 16) | lanes[:, None]
    return compact(valid.reshape(-1), code.reshape(-1), spare, unroll)


def trade(payload):
    return lax.all_to_all(payload, AXES, split_axis=0, concat_axis=0, tiled=True)


def local(positions, smooth, masses, entropy, cell_counts, cell_pairs, pair_count, send_cells):
    cells, tile = smooth.shape
    num_pairs = cell_pairs.shape[1]
    slots = send_cells.shape[1]
    unroll = 32
    targets = send_cells[0]
    padded = (cells + 1, 2, 8, LANES)
    whole = (cells + 1 + slots, 2, 8, LANES)
    pick_m, pick_g = pick_matrix(ROW_MASS), pick_matrix(ROW_G)
    spare = ((cells * CHUNKS) << 16) | cells
    unit = ROWS * TILE * 2000
    both_sems = pltpu.SemaphoreType.DMA((2,))

    own, outgoing = launch(
        prepare_kernel, "prepare", [SMEM, SMEM, VMEM, VMEM, VMEM], [padded, (slots, 2, 8, LANES)],
        (cell_counts, targets, positions, smooth, masses),
    )
    ghosts = trade(outgoing)

    step = jnp.arange(CHUNKS, dtype=jnp.int32)
    ids = jnp.arange(cells, dtype=jnp.int32)
    self_valid = step[None, :] < ((cell_counts + ROWS - 1) // ROWS)[:, None]
    self_code = ((ids[:, None] * CHUNKS + step[None, :]) << 16) | ids[:, None]
    self_units, self_count = compact(self_valid.reshape(-1), self_code.reshape(-1), spare, unroll)
    live_pair = jnp.arange(num_pairs, dtype=jnp.int32) < pair_count[0]
    first, second = cell_pairs[0], cell_pairs[1]
    second = jnp.where(second < cells, second, second + 1)
    inner_units, inner_count = pair_units(first[slots:], second[slots:], live_pair[slots:], cell_counts, spare, unroll)

    (self_rho,) = launch(
        functools.partial(density_inner_kernel, unroll, False), "density_self", [SMEM, SMEM, VMEM, VMEM], [padded],
        (self_count, self_units, own, pick_m), flops=768 * unit,
    )
    ghosts, self_rho = lax.optimization_barrier((ghosts, self_rho))

    ghost_counts = ghosts[:, 0, ROW_G, 0].astype(jnp.int32)
    all_counts = jnp.concatenate([cell_counts, jnp.zeros((1,), jnp.int32), ghost_counts])
    outer_units, outer_count = pair_units(first[:slots], second[:slots], live_pair[:slots], all_counts, spare, unroll)
    outer_rho, ghost_rho = launch(
        functools.partial(density_outer_kernel, unroll), "density_outer", [SMEM, SMEM, ANY, ANY, VMEM],
        [(cells, tile), (slots, 1, tile)], (outer_count, outer_units, own, ghosts, pick_m),
        scratch=[pltpu.VMEM(whole, F32), pltpu.VMEM(whole, F32), both_sems], flops=640 * unit,
    )
    returned_rho = trade(ghost_rho)
    (inner_rho,) = launch(
        functools.partial(density_inner_kernel, unroll, True), "density_inner", [SMEM, SMEM, VMEM, VMEM], [padded],
        (inner_count, inner_units, own, pick_m), flops=320 * unit,
    )
    returned_rho, inner_rho = lax.optimization_barrier((returned_rho, inner_rho))

    density, own_g, outgoing_g = launch(
        factor_kernel, "factor", [SMEM] + [VMEM] * 6, [(cells, tile), padded, (slots, 1, tile)],
        (targets, self_rho, inner_rho, outer_rho, returned_rho, own, entropy),
        scratch=[pltpu.VMEM((cells + 8, tile), F32)] * 3,
    )
    ghost_g = trade(outgoing_g)
    (self_acc,) = launch(
        functools.partial(force_inner_kernel, unroll, False), "force_self", [SMEM, SMEM, VMEM, VMEM], [padded],
        (self_count, self_units, own_g, pick_g), flops=768 * unit,
    )
    ghost_g, self_acc = lax.optimization_barrier((ghost_g, self_acc))

    outer_acc, ghost_acc = launch(
        functools.partial(force_outer_kernel, unroll), "force_outer", [SMEM, SMEM, ANY, ANY, VMEM, VMEM],
        [(cells, 2, 8, LANES), (slots, 2, 4, LANES)], (outer_count, outer_units, own_g, ghosts, ghost_g, pick_g),
        scratch=[pltpu.VMEM(whole, F32), pltpu.VMEM(whole, F32), both_sems], flops=640 * unit,
    )
    returned_acc = trade(ghost_acc)
    (inner_acc,) = launch(
        functools.partial(force_inner_kernel, unroll, True), "force_inner", [SMEM, SMEM, VMEM, VMEM], [padded],
        (inner_count, inner_units, own_g, pick_g), flops=320 * unit,
    )
    returned_acc, inner_acc = lax.optimization_barrier((returned_acc, inner_acc))

    (acceleration,) = launch(
        final_kernel, "final", [SMEM] + [VMEM] * 5, [(3, cells, tile)],
        (targets, self_acc, inner_acc, outer_acc, returned_acc, own), scratch=[pltpu.VMEM(padded, F32)],
    )
    return (density, acceleration)


def solution(mesh):
    in_specs = (
        P(None, AXES, None),
        P(AXES, None),
        P(AXES, None),
        P(AXES, None),
        P(AXES),
        P(None, AXES),
        P(AXES),
        P(AXES, None),
    )
    out_specs = (P(AXES, None), P(None, AXES, None))
    return jax.shard_map(local, mesh=mesh, in_specs=in_specs, out_specs=out_specs, check_vma=False)
```

```python
import functools
import math

import jax
import jax.numpy as jnp
from jax import lax
from jax.experimental import pallas as pl
from jax.experimental.pallas import tpu as pltpu
from jax.sharding import PartitionSpec as P

KERNEL_NORM = 21.0 / (2.0 * math.pi)
AXES = ("gx", "gy")
LANES = 128
TILE = 256
ROWS = 64
CHUNKS = TILE // ROWS
TINY = 1e-30
F32 = jnp.float32
BF16 = jnp.bfloat16

ROW_NORM, ROW_ONE, ROW_H, ROW_MASS, ROW_G = 3, 4, 5, 6, 7

NN = (((1,), (0,)), ((), ()))
TN = (((0,), (0,)), ((), ()))
NT = (((1,), (1,)), ((), ()))


def mxu(a, b, dims):
    return lax.dot_general(a, b, dims, preferred_element_type=F32)


def pieces3(x):
    a = x.astype(BF16).astype(F32)
    r = x - a
    b = r.astype(BF16).astype(F32)
    c = r - b
    return a, b, c


def left_stack(x):
    a, b, c = pieces3(x)
    return jnp.concatenate([a, a, b, b, a, c], axis=0).astype(BF16)


def right_stack(x):
    a, b, c = pieces3(x)
    return jnp.concatenate([a, b, a, b, c, a], axis=0).astype(BF16)


def hi_lo_rows(x):
    hi = x.astype(BF16).astype(F32)
    return jnp.concatenate([hi, x - hi], axis=0).astype(BF16)


def twice(x):
    return jnp.concatenate([x, x], axis=1)


def row_fields(f_ref, i):
    block = f_ref[i >> 2, (i >> 1) & 1]
    return pltpu.roll(block, (i & 1) * ROWS, axis=1)[:, :ROWS]


def lane_fields(f_ref, j):
    return jnp.concatenate([f_ref[j, 0], f_ref[j, 1]], axis=1)


def distances(f_ref, pick, i, j):
    left = left_stack(row_fields(f_ref, i))
    lanes = lane_fields(f_ref, j)
    row = lax.broadcasted_iota(jnp.int32, (8, TILE), 0)
    norm = lanes[ROW_NORM : ROW_NORM + 1, :]
    right = jnp.where(row < 3, -2.0 * lanes, jnp.where(row == ROW_ONE, norm, jnp.where(row == ROW_NORM, 1.0, 0.0)))
    squared = mxu(left, right_stack(right), TN)
    return (squared,) if pick is None else (squared, mxu(left, pick, TN))


def lane_row(f_ref, j, which):
    return jnp.concatenate([f_ref[j, 0, which : which + 1, :], f_ref[j, 1, which : which + 1, :]], axis=1)


def fold_rows(x):
    total = x[0:8]
    for k in range(1, x.shape[0] // 8):
        total = total + x[8 * k : 8 * k + 8]
    return total


def add_lanes(out, j, values):
    out[j, 0] += values[:, :LANES]
    out[j, 1] += values[:, LANES:]


def add_rows(out, i, values):
    lane = lax.broadcasted_iota(jnp.int32, (8, LANES), 1)
    out[i >> 2, (i >> 1) & 1] += jnp.where((lane >> 6) == (i & 1), twice(values), 0.0)


def root(squared):
    squared = jnp.maximum(squared, TINY)
    return squared * lax.rsqrt(squared)


def density_self_values(parts, f_ref, i, j):
    squared, column = parts
    dist = root(squared)
    h = lane_row(f_ref, j, ROW_H)
    t = jnp.maximum(h - dist, 0.0)
    t = t * t
    return fold_rows(t * t * (h + 4.0 * dist) * twice(column))


def density_pair_values(parts, f_ref, i, j):
    squared, column = parts
    dist = root(squared)
    four = 4.0 * dist
    h_row, m_row = twice(column[:, :LANES]), twice(column[:, LANES:])
    h, m = lane_row(f_ref, j, ROW_H), lane_row(f_ref, j, ROW_MASS)
    t = jnp.maximum(h_row - dist, 0.0)
    t = t * t
    near = t * t * (h_row + four) * m
    s = jnp.maximum(h - dist, 0.0)
    s = s * s
    far = s * s * (h + four) * m_row
    return (*hi_lo(near[:, :LANES] + near[:, LANES:]), fold_rows(far))


def density_pair_store(values, out, i, j):
    hi, lo, far = values
    add_lanes(out, j, far)
    one = (lax.broadcasted_iota(jnp.int32, (16, LANES), 0) == 0).astype(BF16)
    add_rows(out, i, (mxu(one, hi, NT) + mxu(one, lo, NT))[0:8])


def hi_lo(x):
    hi = x.astype(BF16)
    return hi, (x - hi.astype(F32)).astype(BF16)


def force_values(parts, f_ref, i, j):
    squared, column = parts
    dist = root(squared)
    h_row, g_row = twice(column[:, :LANES]), twice(column[:, LANES:])
    h, g = lane_row(f_ref, j, ROW_H), lane_row(f_ref, j, ROW_G)
    a = jnp.maximum(h_row - dist, 0.0)
    b = jnp.maximum(h - dist, 0.0)
    return hi_lo(g_row * (a * a * a) + g * (b * b * b))


def moments(x):
    return hi_lo_rows(x * x[ROW_MASS : ROW_MASS + 1, :])


def force_self_values(parts, f_ref, i, j):
    b = jnp.maximum(lane_row(f_ref, j, ROW_H) - root(parts[0]), 0.0)
    return hi_lo(b * b * b)


def force_self_store(values, f_ref, out, i, j):
    hi, lo = values
    g = lane_row(f_ref, j, ROW_G)
    rows = moments(row_fields(f_ref, i))
    add_lanes(out, j, g * fold_rows(mxu(rows, hi, NN) + mxu(rows, lo, NN)))
    lanes = lane_fields(f_ref, j)
    lanes = hi_lo_rows(lanes * (lanes[ROW_MASS : ROW_MASS + 1, :] * g))
    add_rows(out, i, fold_rows(mxu(lanes, hi, NT) + mxu(lanes, lo, NT)))


def force_store(values, f_ref, out, i, j):
    hi, lo = values
    rows = moments(row_fields(f_ref, i))
    add_lanes(out, j, fold_rows(mxu(rows, hi, NN) + mxu(rows, lo, NN)))
    lanes = moments(lane_fields(f_ref, j))
    add_rows(out, i, fold_rows(mxu(lanes, hi, NT) + mxu(lanes, lo, NT)))


def sweep(unroll, lead, lag, count, units, slots, stage_a, stage_b, stage_c):
    part_slots, value_slots = slots

    def unit(index):
        code = units[index]
        return code >> 16, code & 0xFFFF

    def save(refs, k, values):
        for ref, value in zip(refs, values):
            ref[k] = value

    def restore(refs, k):
        return tuple(ref[k] for ref in refs)

    for ref in value_slots:
        ref[...] = jnp.zeros_like(ref)
    for k in range(lead):
        save(part_slots, k, stage_a(*unit(k)))

    def body(step, carry):
        base = step * unroll
        ids = [unit(base + k) for k in range(unroll + lead)]
        behind = [unit(jnp.maximum(base - lag + k, 0)) for k in range(lag)]
        parts = {k: restore(part_slots, k) for k in range(lead)}
        values = {k - lag: restore(value_slots, k) for k in range(lag)}
        for k in range(unroll):
            parts[k + lead] = stage_a(*ids[k + lead])
            values[k] = stage_b(parts.pop(k), *ids[k])
            stage_c(values.pop(k - lag), *(behind[k] if k < lag else ids[k - lag]))
        for k in range(lead):
            save(part_slots, k, parts[unroll + k])
        for k in range(lag):
            save(value_slots, k, values[unroll - lag + k])
        return carry

    lax.fori_loop(0, count, body, 0)
    for k in range(lag):
        stage_c(restore(value_slots, k), *unit(jnp.maximum(count * unroll - lag + k, 0)))


HANDED = {"density_self": (2, 1), "density": (2, 1), "force_self": (2, 2), "force": (2, 1)}


def slot_shapes(kind):
    lead, lag = HANDED[kind]
    parts = [pltpu.VMEM((lead, ROWS, TILE), F32)]
    if kind == "density_self":
        parts.append(pltpu.VMEM((lead, ROWS, LANES), F32))
    elif kind != "force_self":
        parts.append(pltpu.VMEM((lead, ROWS, TILE), F32))
    if kind == "density_self":
        values = [pltpu.VMEM((lag, 8, TILE), F32)]
    elif kind == "density":
        values = [pltpu.VMEM((lag, ROWS, LANES), BF16)] * 2 + [pltpu.VMEM((lag, 8, TILE), F32)]
    else:
        values = [pltpu.VMEM((lag, ROWS, TILE), BF16)] * 2
    return (parts, values)


def sweep_kind(kind, unroll, count, units, f_ref, pick, out, slots):
    picked = {"density_self": pick[:, LANES:], "force_self": None}.get(kind, pick[...])
    middle = {
        "density_self": lambda p, i, j: (density_self_values(p, f_ref, i, j),),
        "density": lambda p, i, j: density_pair_values(p, f_ref, i, j),
        "force_self": lambda p, i, j: force_self_values(p, f_ref, i, j),
        "force": lambda p, i, j: force_values(p, f_ref, i, j),
    }
    last = {
        "density_self": lambda v, i, j: add_lanes(out, j, v[0]),
        "density": lambda v, i, j: density_pair_store(v, out, i, j),
        "force_self": lambda v, i, j: force_self_store(v, f_ref, out, i, j),
        "force": lambda v, i, j: force_store(v, f_ref, out, i, j),
    }
    sweep(
        unroll, *HANDED[kind], count[0], units, slots,
        lambda i, j: distances(f_ref, picked, i, j), middle[kind], last[kind],
    )


def density_scale(h):
    h2 = h * h
    h4 = h2 * h2
    return KERNEL_NORM / (h4 * h4)


def each_group(cells, body):
    def step(k, carry):
        for half in range(2):
            body(pl.multiple_of(k * 8, 8), half)
        return carry

    lax.fori_loop(0, cells // 8, step, 0)


def half_lanes(half):
    return slice(half * LANES, (half + 1) * LANES)


def prepare_kernel(counts, targets, pos, smooth, masses, fields, outgoing, alive):
    cells = smooth.shape[0]
    fields[cells] = jnp.zeros((2, 8, LANES), F32)
    sub = lax.broadcasted_iota(jnp.int32, (8, LANES), 0)
    lane = lax.broadcasted_iota(jnp.int32, (8, LANES), 1)

    def group(c, half):
        count = jnp.zeros((8, LANES), jnp.int32)
        for k in range(8):
            count = jnp.where(sub == k, counts[c + k], count)
        at = (pl.ds(c, 8), half_lanes(half))
        x, y, z = (pos[k, at[0], at[1]] - 0.5 for k in range(3))
        live = lane + half * LANES < count
        alive[at] = jnp.where(live, 1.0, 0.0)
        mass = jnp.where(live, masses[at], 0.0)
        rows = (x, y, z, x * x + y * y + z * z, jnp.ones_like(x), smooth[at], mass, count.astype(F32))
        for k in range(8):
            fields[pl.ds(c, 8), half, k, :] = rows[k]

    each_group(cells, group)

    def export(k, carry):
        for s in range(8):
            slot = k * 8 + s
            outgoing[slot] = fields[jnp.maximum(targets[slot], 0)]
        return carry

    lax.fori_loop(0, outgoing.shape[0] // 8, export, 0)


def load_fields(sources, f_ref, acc, sems):
    copies, first = [], 0
    for k, source in enumerate(sources):
        copies.append(pltpu.make_async_copy(source, f_ref.at[pl.ds(first, source.shape[0])], sems.at[k]))
        first += source.shape[0]
    for copy in copies:
        copy.start()
    acc[...] = jnp.zeros_like(acc)
    for copy in copies:
        copy.wait()


def density_inner_kernel(kind, unroll, count, units, own, pick, out, f_ref, acc, sems, *slots):
    load_fields([own], f_ref, acc, sems)
    sweep_kind(kind, unroll, count, units, f_ref, pick, acc, slots)

    def finish(c, half):
        out[pl.ds(c, 8), half_lanes(half)] = jnp.sum(acc[pl.ds(c, 8), half], axis=1)

    each_group(out.shape[0], finish)


def density_outer_kernel(unroll, count, units, own, ghosts, pick, own_out, ghost_out, f_ref, acc, sems, *slots):
    load_fields([own, ghosts], f_ref, acc, sems)
    sweep_kind("density", unroll, count, units, f_ref, pick, acc, slots)
    first = own.shape[0]

    def finish_own(c, half):
        own_out[pl.ds(c, 8), half_lanes(half)] = jnp.sum(acc[pl.ds(c, 8), half], axis=1)

    def finish_ghost(c, half):
        total = jnp.sum(acc[pl.ds(first + c, 8), half], axis=1)
        scale = density_scale(f_ref[pl.ds(first + c, 8), half, ROW_H, :])
        ghost_out[pl.ds(c, 8), 0, half_lanes(half)] = total * scale

    each_group(own_out.shape[0], finish_own)
    each_group(ghost_out.shape[0], finish_ghost)


def select(targets, cells):
    ids = lax.broadcasted_iota(jnp.int32, (cells, targets.shape[1]), 0)
    return (ids == targets[...]).astype(BF16)


def exact_dot(selector, values, dims):
    a, b, c = (x.astype(BF16) for x in pieces3(values))
    return mxu(selector, a, dims) + mxu(selector, b, dims) + mxu(selector, c, dims)


def factor_kernel(targets, self_rho, inner, outer, returned, alive, smooth, entropy, density, g_out, outgoing):
    cells = density.shape[0]
    selector = select(targets, cells)
    live = alive[...] > 0.0
    scale = density_scale(smooth[...])
    total = (self_rho[...] + inner[...] + outer[...]) * scale + exact_dot(selector, returned[:, 0, :], NN)
    rho = jnp.where(live, total, 0.0)
    density[...] = rho
    safe = jnp.where(live, rho, 1.0)
    g = jnp.where(live, entropy[...] * jnp.exp(jnp.log(safe) * (-1.0 / 3.0)) * (20.0 * scale), 0.0)
    g_out[...] = g
    outgoing[:, 0, :] = exact_dot(selector, g, TN)


def insert_g(f_ref, g, first, load):
    def body(c, half):
        f_ref[pl.ds(first + c, 8), half, ROW_G, :] = load(g, c, half)

    each_group(g.shape[0], body)


def natural(g, c, half):
    return g[pl.ds(c, 8), half_lanes(half)]


def by_slot(g, c, half):
    return g[pl.ds(c, 8), 0, half_lanes(half)]


def finish_force(f_ref, acc, out):
    def body(c, half):
        def row(ref, k):
            return ref[pl.ds(c, 8), half, k, :]

        live = row(f_ref, ROW_MASS) > 0.0
        total = row(acc, ROW_ONE)
        for k in range(3):
            out[k, pl.ds(c, 8), half_lanes(half)] = jnp.where(live, row(f_ref, k) * total - row(acc, k), 0.0)

    each_group(out.shape[1], body)


def force_inner_kernel(kind, unroll, count, units, own, own_g, pick, out, f_ref, acc, sems, *slots):
    load_fields([own], f_ref, acc, sems)
    insert_g(f_ref, own_g, 0, natural)
    sweep_kind(kind, unroll, count, units, f_ref, pick, acc, slots)
    finish_force(f_ref, acc, out)


def force_outer_kernel(unroll, count, units, own, ghosts, own_g, ghost_g, pick, own_out, ghost_out, f_ref, acc, sems, *slots):
    load_fields([own, ghosts], f_ref, acc, sems)
    first = own.shape[0]
    insert_g(f_ref, own_g, 0, natural)
    insert_g(f_ref, ghost_g, first, by_slot)
    sweep_kind("force", unroll, count, units, f_ref, pick, acc, slots)
    finish_force(f_ref, acc, own_out)

    def finish(k, carry):
        for s in range(4):
            for half in range(2):
                f, sums = f_ref[first + 4 * k + s, half], acc[first + 4 * k + s, half]
                live = f[ROW_MASS : ROW_MASS + 1, :] > 0.0
                ghost_out[4 * k + s, half] = jnp.where(live, f * sums[ROW_ONE : ROW_ONE + 1, :] - sums, 0.0)[0:4]
        return carry

    lax.fori_loop(0, ghost_out.shape[0] // 4, finish, 0)


def final_kernel(targets, self_acc, inner_acc, outer_acc, returned, acceleration):
    selector = select(targets, acceleration.shape[1])
    for half in range(2):
        lanes = half_lanes(half)
        for k in range(3):
            here = self_acc[k, :, lanes] + inner_acc[k, :, lanes] + outer_acc[k, :, lanes]
            acceleration[k, :, lanes] = here + exact_dot(selector, returned[:, half, k, :], NN)


SMEM = pl.BlockSpec(memory_space=pltpu.SMEM)
VMEM = pl.BlockSpec(memory_space=pltpu.VMEM)
ANY = pl.BlockSpec(memory_space=pl.ANY)


def launch(body, name, in_specs, shapes, args, scratch=(), flops=0, limit=40):
    return pl.pallas_call(
        body,
        out_shape=[jax.ShapeDtypeStruct(shape, F32) for shape in shapes],
        in_specs=in_specs,
        out_specs=[VMEM] * len(shapes),
        scratch_shapes=list(scratch),
        name=name,
        compiler_params=pltpu.CompilerParams(vmem_limit_bytes=limit * 1024 * 1024),
        cost_estimate=pl.CostEstimate(flops=flops, bytes_accessed=1 << 21, transcendentals=0),
    )(*args)


def pick_matrix(second):
    k = lax.broadcasted_iota(jnp.int32, (48, TILE), 0)
    lane = lax.broadcasted_iota(jnp.int32, (48, TILE), 1)
    group, row = k // 8, k % 8
    used = (group == 0) | (group == 2) | (group == 5)
    return (used & (row == jnp.where(lane < LANES, ROW_H, second))).astype(BF16)


def compact(valid, code, spare, unroll):
    num = valid.shape[0]
    flags = valid.astype(jnp.int32)
    ids = jnp.arange(num, dtype=jnp.int32)
    rank = jnp.sum(jnp.where(ids[None, :] < ids[:, None], flags[None, :], 0), axis=1)
    total = jnp.sum(flags)
    hit = (rank[None, :] == ids[:, None]) & valid[None, :]
    listed = jnp.sum(jnp.where(hit, code[None, :], 0), axis=1)
    listed = jnp.where(ids < total, listed, spare)
    listed = jnp.concatenate([listed, jnp.full((LANES,), spare, listed.dtype)])
    return listed.astype(jnp.int32), ((total + unroll - 1) // unroll).reshape(1).astype(jnp.int32)


def look_up(table, ids):
    slots = jnp.arange(table.shape[0], dtype=jnp.int32)
    return jnp.sum(jnp.where(ids[:, None] == slots[None, :], table[None, :], 0), axis=1)


def pair_units(first, second, live, counts, spare, unroll):
    n_first, n_second = look_up(counts, first), look_up(counts, second)
    swap = n_second < n_first
    rows = jnp.where(swap, second, first)
    lanes = jnp.where(swap, first, second)
    chunks = (jnp.minimum(n_first, n_second) + ROWS - 1) // ROWS
    step = jnp.arange(CHUNKS, dtype=jnp.int32)
    valid = (step[None, :] < chunks[:, None]) & live[:, None]
    code = ((rows[:, None] * CHUNKS + step[None, :]) << 16) | lanes[:, None]
    return compact(valid.reshape(-1), code.reshape(-1), spare, unroll)


def trade(payload):
    return lax.all_to_all(payload, AXES, split_axis=0, concat_axis=0, tiled=True)


def local(positions, smooth, masses, entropy, cell_counts, cell_pairs, pair_count, send_cells):
    cells, tile = smooth.shape
    num_pairs = cell_pairs.shape[1]
    slots = send_cells.shape[1]
    unroll = 32
    targets = send_cells[0]
    padded = (cells + 1, 2, 8, LANES)
    whole = (cells + 1 + slots, 2, 8, LANES)
    pick_m, pick_g = pick_matrix(ROW_MASS), pick_matrix(ROW_G)
    spare = ((cells * CHUNKS) << 16) | cells
    unit = ROWS * TILE * 2000
    both_sems = pltpu.SemaphoreType.DMA((2,))

    own, outgoing, alive = launch(
        prepare_kernel, "prepare", [SMEM, SMEM, VMEM, VMEM, VMEM], [padded, (slots, 2, 8, LANES), (cells, tile)],
        (cell_counts, targets, positions, smooth, masses),
    )
    ghosts = trade(outgoing)

    step = jnp.arange(CHUNKS, dtype=jnp.int32)
    ids = jnp.arange(cells, dtype=jnp.int32)
    self_valid = step[None, :] < ((cell_counts + ROWS - 1) // ROWS)[:, None]
    self_code = ((ids[:, None] * CHUNKS + step[None, :]) << 16) | ids[:, None]
    self_units, self_count = compact(self_valid.reshape(-1), self_code.reshape(-1), spare, unroll)
    live_pair = jnp.arange(num_pairs, dtype=jnp.int32) < pair_count[0]
    first, second = cell_pairs[0], cell_pairs[1]
    second = jnp.where(second < cells, second, second + 1)
    inner_units, inner_count = pair_units(first[slots:], second[slots:], live_pair[slots:], cell_counts, spare, unroll)

    def scratch(shape, kind):
        return [pltpu.VMEM(shape, F32), pltpu.VMEM(shape, F32), both_sems, *slot_shapes(kind)]

    (self_rho,) = launch(
        functools.partial(density_inner_kernel, "density_self", unroll), "density_self", [SMEM, SMEM, ANY, VMEM],
        [(cells, tile)], (self_count, self_units, own, pick_m), scratch(padded, "density_self"), 768 * unit,
    )
    ghosts, self_rho = lax.optimization_barrier((ghosts, self_rho))

    ghost_counts = jnp.max(ghosts[:, 0, ROW_G, :], axis=-1).astype(jnp.int32)
    all_counts = jnp.concatenate([cell_counts, jnp.zeros((1,), jnp.int32), ghost_counts])
    outer_units, outer_count = pair_units(first[:slots], second[:slots], live_pair[:slots], all_counts, spare, unroll)
    outer_rho, ghost_rho = launch(
        functools.partial(density_outer_kernel, unroll), "density_outer", [SMEM, SMEM, ANY, ANY, VMEM],
        [(cells, tile), (slots, 1, tile)], (outer_count, outer_units, own, ghosts, pick_m),
        scratch(whole, "density"), 640 * unit,
    )
    returned_rho = trade(ghost_rho)
    (inner_rho,) = launch(
        functools.partial(density_inner_kernel, "density", unroll), "density_inner", [SMEM, SMEM, ANY, VMEM],
        [(cells, tile)], (inner_count, inner_units, own, pick_m), scratch(padded, "density"), 320 * unit,
    )
    returned_rho, inner_rho = lax.optimization_barrier((returned_rho, inner_rho))

    density, own_g, outgoing_g = launch(
        factor_kernel, "factor", [VMEM] * 8, [(cells, tile), (cells, tile), (slots, 1, tile)],
        (send_cells, self_rho, inner_rho, outer_rho, returned_rho, alive, smooth, entropy),
    )
    ghost_g = trade(outgoing_g)
    (self_acc,) = launch(
        functools.partial(force_inner_kernel, "force_self", unroll), "force_self", [SMEM, SMEM, ANY, VMEM, VMEM],
        [(3, cells, tile)], (self_count, self_units, own, own_g, pick_g), scratch(padded, "force_self"), 768 * unit,
    )
    ghost_g, self_acc = lax.optimization_barrier((ghost_g, self_acc))

    outer_acc, ghost_acc = launch(
        functools.partial(force_outer_kernel, unroll), "force_outer", [SMEM, SMEM, ANY, ANY, VMEM, VMEM, VMEM],
        [(3, cells, tile), (slots, 2, 4, LANES)], (outer_count, outer_units, own, ghosts, own_g, ghost_g, pick_g),
        scratch(whole, "force"), 640 * unit,
    )
    returned_acc = trade(ghost_acc)
    (inner_acc,) = launch(
        functools.partial(force_inner_kernel, "force", unroll), "force_inner", [SMEM, SMEM, ANY, VMEM, VMEM],
        [(3, cells, tile)], (inner_count, inner_units, own, own_g, pick_g), scratch(padded, "force"), 320 * unit,
    )
    returned_acc, inner_acc = lax.optimization_barrier((returned_acc, inner_acc))

    (acceleration,) = launch(
        final_kernel, "final", [VMEM] * 5, [(3, cells, tile)],
        (send_cells, self_acc, inner_acc, outer_acc, returned_acc),
    )
    return (density, acceleration)


def solution(mesh):
    in_specs = (
        P(None, AXES, None),
        P(AXES, None),
        P(AXES, None),
        P(AXES, None),
        P(AXES),
        P(None, AXES),
        P(AXES),
        P(AXES, None),
    )
    out_specs = (P(AXES, None), P(None, AXES, None))
    return jax.shard_map(local, mesh=mesh, in_specs=in_specs, out_specs=out_specs, check_vma=False)
```

```python
import functools
import math

import jax
import jax.numpy as jnp
from jax import lax
from jax.experimental import pallas as pl
from jax.experimental.pallas import tpu as pltpu
from jax.sharding import PartitionSpec as P

KERNEL_NORM = 21.0 / (2.0 * math.pi)
AXES = ("gx", "gy")
LANES = 128
TILE = 256
ROWS = 64
CHUNKS = TILE // ROWS
TINY = 1e-30
F32 = jnp.float32
BF16 = jnp.bfloat16

ROW_NORM, ROW_ONE, ROW_H, ROW_MASS, ROW_G = 3, 4, 5, 6, 7

NN = (((1,), (0,)), ((), ()))
TN = (((0,), (0,)), ((), ()))
NT = (((1,), (1,)), ((), ()))


def mxu(a, b, dims):
    return lax.dot_general(a, b, dims, preferred_element_type=F32)


def pieces3(x):
    a = x.astype(BF16).astype(F32)
    r = x - a
    b = r.astype(BF16).astype(F32)
    c = r - b
    return a, b, c


def left_stack(x):
    a, b, c = pieces3(x)
    return jnp.concatenate([a, a, b, b, a, c], axis=0).astype(BF16)


def right_stack(x):
    a, b, c = pieces3(x)
    return jnp.concatenate([a, b, a, b, c, a], axis=0).astype(BF16)


def hi_lo_rows(x):
    hi = x.astype(BF16).astype(F32)
    return jnp.concatenate([hi, x - hi], axis=0).astype(BF16)


def twice(x):
    return jnp.concatenate([x, x], axis=1)


def row_fields(f_ref, i):
    block = f_ref[i >> 2, (i >> 1) & 1]
    return pltpu.roll(block, (i & 1) * ROWS, axis=1)[:, :ROWS]


def lane_fields(f_ref, j):
    return jnp.concatenate([f_ref[j, 0], f_ref[j, 1]], axis=1)


def distances(f_ref, pick, i, j):
    left = left_stack(row_fields(f_ref, i))
    lanes = lane_fields(f_ref, j)
    row = lax.broadcasted_iota(jnp.int32, (8, TILE), 0)
    norm = lanes[ROW_NORM : ROW_NORM + 1, :]
    right = jnp.where(row < 3, -32.0 * lanes, jnp.where(row == ROW_ONE, 16.0 * norm, jnp.where(row == ROW_NORM, 16.0, 0.0)))
    squared = mxu(left, right_stack(right), TN)
    return (squared,) if pick is None else (squared, mxu(left, pick, TN))


def lane_row(f_ref, j, which):
    return jnp.concatenate([f_ref[j, 0, which : which + 1, :], f_ref[j, 1, which : which + 1, :]], axis=1)


def fold_rows(x):
    total = x[0:8]
    for k in range(1, x.shape[0] // 8):
        total = total + x[8 * k : 8 * k + 8]
    return total


def add_lanes(out, j, values):
    out[j, 0] += values[:, :LANES]
    out[j, 1] += values[:, LANES:]


def add_rows(out, i, values):
    lane = lax.broadcasted_iota(jnp.int32, (8, LANES), 1)
    out[i >> 2, (i >> 1) & 1] += jnp.where((lane >> 6) == (i & 1), twice(values), 0.0)


def root(squared):
    squared = jnp.maximum(squared, TINY)
    return squared * lax.rsqrt(squared)


def density_self_values(parts, f_ref, i, j):
    squared, column = parts
    dist = root(squared)
    h = lane_row(f_ref, j, ROW_H)
    t = jnp.maximum(4.0 * h - dist, 0.0)
    t = t * t
    return fold_rows(t * t * (h + dist) * twice(column))


def density_pair_values(parts, f_ref, i, j):
    squared, column = parts
    dist = root(squared)
    h_row, m_row = twice(column[:, :LANES]), twice(column[:, LANES:])
    quarter = twice(0.25 * column[:, :LANES])
    h, m = lane_row(f_ref, j, ROW_H), lane_row(f_ref, j, ROW_MASS)
    t = jnp.maximum(h_row - dist, 0.0)
    t = t * t
    near = t * t * (quarter + dist) * m
    s = jnp.maximum(4.0 * h - dist, 0.0)
    s = s * s
    far = s * s * (h + dist) * m_row
    return (*hi_lo(near[:, :LANES] + near[:, LANES:]), fold_rows(far))


def density_pair_store(values, out, i, j):
    hi, lo, far = values
    add_lanes(out, j, far)
    one = (lax.broadcasted_iota(jnp.int32, (16, LANES), 0) == 0).astype(BF16)
    add_rows(out, i, (mxu(one, hi, NT) + mxu(one, lo, NT))[0:8])


def hi_lo(x):
    hi = x.astype(BF16)
    return hi, (x - hi.astype(F32)).astype(BF16)


def force_values(parts, f_ref, i, j):
    squared, column = parts
    dist = root(squared)
    h_row, g_row = twice(column[:, :LANES]), twice(column[:, LANES:])
    h, g = lane_row(f_ref, j, ROW_H), lane_row(f_ref, j, ROW_G)
    a = jnp.maximum(h_row - dist, 0.0)
    b = jnp.maximum(4.0 * h - dist, 0.0)
    return hi_lo(g_row * (a * a * a) + g * (b * b * b))


def moments(x):
    return hi_lo_rows(x * x[ROW_MASS : ROW_MASS + 1, :])


def force_self_values(parts, f_ref, i, j):
    b = jnp.maximum(4.0 * lane_row(f_ref, j, ROW_H) - root(parts[0]), 0.0)
    return hi_lo(b * b * b)


def force_self_store(values, f_ref, out, i, j):
    hi, lo = values
    g = lane_row(f_ref, j, ROW_G)
    rows = moments(row_fields(f_ref, i))
    add_lanes(out, j, g * fold_rows(mxu(rows, hi, NN) + mxu(rows, lo, NN)))
    lanes = lane_fields(f_ref, j)
    lanes = hi_lo_rows(lanes * (lanes[ROW_MASS : ROW_MASS + 1, :] * g))
    add_rows(out, i, fold_rows(mxu(lanes, hi, NT) + mxu(lanes, lo, NT)))


def force_store(values, f_ref, out, i, j):
    hi, lo = values
    rows = moments(row_fields(f_ref, i))
    add_lanes(out, j, fold_rows(mxu(rows, hi, NN) + mxu(rows, lo, NN)))
    lanes = moments(lane_fields(f_ref, j))
    add_rows(out, i, fold_rows(mxu(lanes, hi, NT) + mxu(lanes, lo, NT)))


def sweep(unroll, lead, lag, count, units, slots, stage_a, stage_b, stage_c):
    part_slots, value_slots = slots

    def unit(index):
        code = units[index]
        return code >> 16, code & 0xFFFF

    def save(refs, k, values):
        for ref, value in zip(refs, values):
            ref[k] = value

    def restore(refs, k):
        return tuple(ref[k] for ref in refs)

    for ref in value_slots:
        ref[...] = jnp.zeros_like(ref)
    for k in range(lead):
        save(part_slots, k, stage_a(*unit(k)))

    def body(step, carry):
        base = step * unroll
        ids = [unit(base + k) for k in range(unroll + lead)]
        behind = [unit(jnp.maximum(base - lag + k, 0)) for k in range(lag)]
        parts = {k: restore(part_slots, k) for k in range(lead)}
        values = {k - lag: restore(value_slots, k) for k in range(lag)}
        for k in range(unroll):
            parts[k + lead] = stage_a(*ids[k + lead])
            values[k] = stage_b(parts.pop(k), *ids[k])
            stage_c(values.pop(k - lag), *(behind[k] if k < lag else ids[k - lag]))
        for k in range(lead):
            save(part_slots, k, parts[unroll + k])
        for k in range(lag):
            save(value_slots, k, values[unroll - lag + k])
        return carry

    lax.fori_loop(0, count, body, 0)
    for k in range(lag):
        stage_c(restore(value_slots, k), *unit(jnp.maximum(count * unroll - lag + k, 0)))


HANDED = {"density_self": (2, 1), "density": (2, 1), "force_self": (2, 2), "force": (2, 1)}


def slot_shapes(kind):
    lead, lag = HANDED[kind]
    parts = [pltpu.VMEM((lead, ROWS, TILE), F32)]
    if kind == "density_self":
        parts.append(pltpu.VMEM((lead, ROWS, LANES), F32))
    elif kind != "force_self":
        parts.append(pltpu.VMEM((lead, ROWS, TILE), F32))
    if kind == "density_self":
        values = [pltpu.VMEM((lag, 8, TILE), F32)]
    elif kind == "density":
        values = [pltpu.VMEM((lag, ROWS, LANES), BF16)] * 2 + [pltpu.VMEM((lag, 8, TILE), F32)]
    else:
        values = [pltpu.VMEM((lag, ROWS, TILE), BF16)] * 2
    return (parts, values)


def sweep_kind(kind, unroll, count, units, f_ref, pick, out, slots):
    picked = {"density_self": pick[:, LANES:], "force_self": None}.get(kind, pick[...])
    middle = {
        "density_self": lambda p, i, j: (density_self_values(p, f_ref, i, j),),
        "density": lambda p, i, j: density_pair_values(p, f_ref, i, j),
        "force_self": lambda p, i, j: force_self_values(p, f_ref, i, j),
        "force": lambda p, i, j: force_values(p, f_ref, i, j),
    }
    last = {
        "density_self": lambda v, i, j: add_lanes(out, j, v[0]),
        "density": lambda v, i, j: density_pair_store(v, out, i, j),
        "force_self": lambda v, i, j: force_self_store(v, f_ref, out, i, j),
        "force": lambda v, i, j: force_store(v, f_ref, out, i, j),
    }
    sweep(
        unroll, *HANDED[kind], count[0], units, slots,
        lambda i, j: distances(f_ref, picked, i, j), middle[kind], last[kind],
    )


def density_scale(h):
    h2 = h * h
    h4 = h2 * h2
    return KERNEL_NORM / 256.0 / (h4 * h4)


def each_group(cells, body):
    def step(k, carry):
        for half in range(2):
            body(pl.multiple_of(k * 8, 8), half)
        return carry

    lax.fori_loop(0, cells // 8, step, 0)


def half_lanes(half):
    return slice(half * LANES, (half + 1) * LANES)


def prepare_kernel(counts, targets, pos, smooth, masses, fields, outgoing, alive):
    cells = smooth.shape[0]
    fields[cells] = jnp.zeros((2, 8, LANES), F32)
    sub = lax.broadcasted_iota(jnp.int32, (8, LANES), 0)
    lane = lax.broadcasted_iota(jnp.int32, (8, LANES), 1)

    def group(c, half):
        count = jnp.zeros((8, LANES), jnp.int32)
        for k in range(8):
            count = jnp.where(sub == k, counts[c + k], count)
        at = (pl.ds(c, 8), half_lanes(half))
        x, y, z = (pos[k, at[0], at[1]] - 0.5 for k in range(3))
        live = lane + half * LANES < count
        alive[at] = jnp.where(live, 1.0, 0.0)
        mass = jnp.where(live, masses[at], 0.0)
        rows = (x, y, z, x * x + y * y + z * z, jnp.ones_like(x), smooth[at], mass, count.astype(F32))
        for k in range(8):
            fields[pl.ds(c, 8), half, k, :] = rows[k]

    each_group(cells, group)

    def export(k, carry):
        for s in range(8):
            slot = k * 8 + s
            outgoing[slot] = fields[jnp.maximum(targets[slot], 0)]
        return carry

    lax.fori_loop(0, outgoing.shape[0] // 8, export, 0)


def load_fields(sources, f_ref, acc, sems):
    copies, first = [], 0
    for k, source in enumerate(sources):
        copies.append(pltpu.make_async_copy(source, f_ref.at[pl.ds(first, source.shape[0])], sems.at[k]))
        first += source.shape[0]
    for copy in copies:
        copy.start()
    acc[...] = jnp.zeros_like(acc)
    for copy in copies:
        copy.wait()


def density_inner_kernel(kind, unroll, count, units, f_ref, pick, out, acc, *slots):
    acc[...] = jnp.zeros_like(acc)
    sweep_kind(kind, unroll, count, units, f_ref, pick, acc, slots)

    def finish(c, half):
        out[pl.ds(c, 8), half_lanes(half)] = jnp.sum(acc[pl.ds(c, 8), half], axis=1)

    each_group(out.shape[0], finish)


def density_outer_kernel(unroll, count, units, own, ghosts, pick, own_out, ghost_out, f_ref, acc, sems, *slots):
    load_fields([own, ghosts], f_ref, acc, sems)
    sweep_kind("density", unroll, count, units, f_ref, pick, acc, slots)
    first = own.shape[0]

    def finish_own(c, half):
        own_out[pl.ds(c, 8), half_lanes(half)] = jnp.sum(acc[pl.ds(c, 8), half], axis=1)

    def finish_ghost(c, half):
        total = jnp.sum(acc[pl.ds(first + c, 8), half], axis=1)
        scale = density_scale(f_ref[pl.ds(first + c, 8), half, ROW_H, :])
        ghost_out[pl.ds(c, 8), 0, half_lanes(half)] = total * scale

    each_group(own_out.shape[0], finish_own)
    each_group(ghost_out.shape[0], finish_ghost)


def select(targets, cells):
    ids = lax.broadcasted_iota(jnp.int32, (cells, targets.shape[1]), 0)
    return (ids == targets[...]).astype(BF16)


def exact_dot(selector, values, dims):
    a, b, c = (x.astype(BF16) for x in pieces3(values))
    return mxu(selector, a, dims) + mxu(selector, b, dims) + mxu(selector, c, dims)


def factor_kernel(targets, self_rho, inner, outer, returned, alive, smooth, entropy, density, g_out, outgoing):
    cells = density.shape[0]
    selector = select(targets, cells)
    live = alive[...] > 0.0
    scale = density_scale(smooth[...])
    total = (self_rho[...] + inner[...] + outer[...]) * scale + exact_dot(selector, returned[:, 0, :], NN)
    rho = jnp.where(live, total, 0.0)
    density[...] = rho
    safe = jnp.where(live, rho, 1.0)
    g = jnp.where(live, entropy[...] * jnp.exp(jnp.log(safe) * (-1.0 / 3.0)) * (80.0 * scale), 0.0)
    g_out[...] = g
    outgoing[:, 0, :] = exact_dot(selector, g, TN)


def insert_g(f_ref, g, first, load):
    def body(c, half):
        f_ref[pl.ds(first + c, 8), half, ROW_G, :] = load(g, c, half)

    each_group(g.shape[0], body)


def natural(g, c, half):
    return g[pl.ds(c, 8), half_lanes(half)]


def by_slot(g, c, half):
    return g[pl.ds(c, 8), 0, half_lanes(half)]


def finish_force(f_ref, acc, out):
    def body(c, half):
        def row(ref, k):
            return ref[pl.ds(c, 8), half, k, :]

        live = row(f_ref, ROW_MASS) > 0.0
        total = row(acc, ROW_ONE)
        for k in range(3):
            out[k, pl.ds(c, 8), half_lanes(half)] = jnp.where(live, row(f_ref, k) * total - row(acc, k), 0.0)

    each_group(out.shape[1], body)


def force_inner_kernel(kind, unroll, count, units, own, own_g, pick, out, f_ref, acc, sems, *slots):
    load_fields([own], f_ref, acc, sems)
    insert_g(f_ref, own_g, 0, natural)
    sweep_kind(kind, unroll, count, units, f_ref, pick, acc, slots)
    finish_force(f_ref, acc, out)


def force_outer_kernel(unroll, count, units, own, ghosts, own_g, ghost_g, pick, own_out, ghost_out, f_ref, acc, sems, *slots):
    load_fields([own, ghosts], f_ref, acc, sems)
    first = own.shape[0]
    insert_g(f_ref, own_g, 0, natural)
    insert_g(f_ref, ghost_g, first, by_slot)
    sweep_kind("force", unroll, count, units, f_ref, pick, acc, slots)
    finish_force(f_ref, acc, own_out)

    def finish(k, carry):
        for s in range(4):
            for half in range(2):
                f, sums = f_ref[first + 4 * k + s, half], acc[first + 4 * k + s, half]
                live = f[ROW_MASS : ROW_MASS + 1, :] > 0.0
                ghost_out[4 * k + s, half] = jnp.where(live, f * sums[ROW_ONE : ROW_ONE + 1, :] - sums, 0.0)[0:4]
        return carry

    lax.fori_loop(0, ghost_out.shape[0] // 4, finish, 0)


def final_kernel(targets, self_acc, inner_acc, outer_acc, returned, acceleration):
    selector = select(targets, acceleration.shape[1])
    for half in range(2):
        lanes = half_lanes(half)
        for k in range(3):
            here = self_acc[k, :, lanes] + inner_acc[k, :, lanes] + outer_acc[k, :, lanes]
            acceleration[k, :, lanes] = here + exact_dot(selector, returned[:, half, k, :], NN)


SMEM = pl.BlockSpec(memory_space=pltpu.SMEM)
VMEM = pl.BlockSpec(memory_space=pltpu.VMEM)
ANY = pl.BlockSpec(memory_space=pl.ANY)


def launch(body, name, in_specs, shapes, args, scratch=(), flops=0, limit=40):
    return pl.pallas_call(
        body,
        out_shape=[jax.ShapeDtypeStruct(shape, F32) for shape in shapes],
        in_specs=in_specs,
        out_specs=[VMEM] * len(shapes),
        scratch_shapes=list(scratch),
        name=name,
        compiler_params=pltpu.CompilerParams(vmem_limit_bytes=limit * 1024 * 1024),
        cost_estimate=pl.CostEstimate(flops=flops, bytes_accessed=1 << 21, transcendentals=0),
    )(*args)


def pick_matrix(second):
    k = lax.broadcasted_iota(jnp.int32, (48, TILE), 0)
    lane = lax.broadcasted_iota(jnp.int32, (48, TILE), 1)
    group, row = k // 8, k % 8
    used = (group == 0) | (group == 2) | (group == 5)
    weight = jnp.where(lane < LANES, 4.0, 1.0)
    return jnp.where(used & (row == jnp.where(lane < LANES, ROW_H, second)), weight, 0.0).astype(BF16)


def compact(valid, code, spare, unroll):
    num = valid.shape[0]
    flags = valid.astype(jnp.int32)
    ids = jnp.arange(num, dtype=jnp.int32)
    rank = jnp.sum(jnp.where(ids[None, :] < ids[:, None], flags[None, :], 0), axis=1)
    total = jnp.sum(flags)
    hit = (rank[None, :] == ids[:, None]) & valid[None, :]
    listed = jnp.sum(jnp.where(hit, code[None, :], 0), axis=1)
    listed = jnp.where(ids < total, listed, spare)
    listed = jnp.concatenate([listed, jnp.full((LANES,), spare, listed.dtype)])
    return listed.astype(jnp.int32), ((total + unroll - 1) // unroll).reshape(1).astype(jnp.int32)


def look_up(table, ids):
    slots = jnp.arange(table.shape[0], dtype=jnp.int32)
    return jnp.sum(jnp.where(ids[:, None] == slots[None, :], table[None, :], 0), axis=1)


def pair_units(first, second, live, counts, spare, unroll):
    n_first, n_second = look_up(counts, first), look_up(counts, second)
    swap = n_second < n_first
    rows = jnp.where(swap, second, first)
    lanes = jnp.where(swap, first, second)
    chunks = (jnp.minimum(n_first, n_second) + ROWS - 1) // ROWS
    step = jnp.arange(CHUNKS, dtype=jnp.int32)
    valid = (step[None, :] < chunks[:, None]) & live[:, None]
    code = ((rows[:, None] * CHUNKS + step[None, :]) << 16) | lanes[:, None]
    return compact(valid.reshape(-1), code.reshape(-1), spare, unroll)


def trade(payload):
    peers = lax.axis_size(AXES)
    by_peer = payload.reshape(peers, -1, *payload.shape[2:-1], LANES)
    return lax.all_to_all(by_peer, AXES, split_axis=0, concat_axis=0, tiled=True).reshape(payload.shape)


def local(positions, smooth, masses, entropy, cell_counts, cell_pairs, pair_count, send_cells):
    cells, tile = smooth.shape
    num_pairs = cell_pairs.shape[1]
    slots = send_cells.shape[1]
    unroll = 32
    targets = send_cells[0]
    padded = (cells + 1, 2, 8, LANES)
    whole = (cells + 1 + slots, 2, 8, LANES)
    pick_m, pick_g = pick_matrix(ROW_MASS), pick_matrix(ROW_G)
    spare = ((cells * CHUNKS) << 16) | cells
    unit = ROWS * TILE * 2000
    both_sems = pltpu.SemaphoreType.DMA((2,))

    own, outgoing, alive = launch(
        prepare_kernel, "prepare", [SMEM, SMEM, VMEM, VMEM, VMEM], [padded, (slots, 2, 8, LANES), (cells, tile)],
        (cell_counts, targets, positions, smooth, masses),
    )
    ghosts = trade(outgoing)

    step = jnp.arange(CHUNKS, dtype=jnp.int32)
    ids = jnp.arange(cells, dtype=jnp.int32)
    self_valid = step[None, :] < ((cell_counts + ROWS - 1) // ROWS)[:, None]
    self_code = ((ids[:, None] * CHUNKS + step[None, :]) << 16) | ids[:, None]
    self_units, self_count = compact(self_valid.reshape(-1), self_code.reshape(-1), spare, unroll)
    live_pair = jnp.arange(num_pairs, dtype=jnp.int32) < pair_count[0]
    first, second = cell_pairs[0], cell_pairs[1]
    second = jnp.where(second < cells, second, second + 1)
    inner_units, inner_count = pair_units(first[slots:], second[slots:], live_pair[slots:], cell_counts, spare, unroll)

    def scratch(shape, kind):
        return [pltpu.VMEM(shape, F32), pltpu.VMEM(shape, F32), both_sems, *slot_shapes(kind)]

    (self_rho,) = launch(
        functools.partial(density_inner_kernel, "density_self", unroll), "density_self", [SMEM, SMEM, VMEM, VMEM],
        [(cells, tile)], (self_count, self_units, own, pick_m), [pltpu.VMEM(padded, F32), *slot_shapes("density_self")], 768 * unit,
    )
    ghosts, self_rho = lax.optimization_barrier((ghosts, self_rho))

    ghost_counts = jnp.max(ghosts[:, 0, ROW_G, :], axis=-1).astype(jnp.int32)
    all_counts = jnp.concatenate([cell_counts, jnp.zeros((1,), jnp.int32), ghost_counts])
    outer_units, outer_count = pair_units(first[:slots], second[:slots], live_pair[:slots], all_counts, spare, unroll)
    outer_rho, ghost_rho = launch(
        functools.partial(density_outer_kernel, unroll), "density_outer", [SMEM, SMEM, ANY, ANY, VMEM],
        [(cells, tile), (slots, 1, tile)], (outer_count, outer_units, own, ghosts, pick_m),
        scratch(whole, "density"), 640 * unit,
    )
    returned_rho = trade(ghost_rho)
    (inner_rho,) = launch(
        functools.partial(density_inner_kernel, "density", unroll), "density_inner", [SMEM, SMEM, VMEM, VMEM],
        [(cells, tile)], (inner_count, inner_units, own, pick_m), [pltpu.VMEM(padded, F32), *slot_shapes("density")], 320 * unit,
    )
    returned_rho, inner_rho = lax.optimization_barrier((returned_rho, inner_rho))

    density, own_g, outgoing_g = launch(
        factor_kernel, "factor", [VMEM] * 8, [(cells, tile), (cells, tile), (slots, 1, tile)],
        (send_cells, self_rho, inner_rho, outer_rho, returned_rho, alive, smooth, entropy),
    )
    ghost_g = trade(outgoing_g)
    (self_acc,) = launch(
        functools.partial(force_inner_kernel, "force_self", unroll), "force_self", [SMEM, SMEM, ANY, VMEM, VMEM],
        [(3, cells, tile)], (self_count, self_units, own, own_g, pick_g), scratch(padded, "force_self"), 768 * unit,
    )
    ghost_g, self_acc = lax.optimization_barrier((ghost_g, self_acc))

    outer_acc, ghost_acc = launch(
        functools.partial(force_outer_kernel, unroll), "force_outer", [SMEM, SMEM, ANY, ANY, VMEM, VMEM, VMEM],
        [(3, cells, tile), (slots, 2, 4, LANES)], (outer_count, outer_units, own, ghosts, own_g, ghost_g, pick_g),
        scratch(whole, "force"), 640 * unit,
    )
    returned_acc = trade(ghost_acc)
    (inner_acc,) = launch(
        functools.partial(force_inner_kernel, "force", unroll), "force_inner", [SMEM, SMEM, ANY, VMEM, VMEM],
        [(3, cells, tile)], (inner_count, inner_units, own, own_g, pick_g), scratch(padded, "force"), 320 * unit,
    )
    returned_acc, inner_acc = lax.optimization_barrier((returned_acc, inner_acc))

    (acceleration,) = launch(
        final_kernel, "final", [VMEM] * 5, [(3, cells, tile)],
        (send_cells, self_acc, inner_acc, outer_acc, returned_acc),
    )
    return (density, acceleration)


def solution(mesh):
    in_specs = (
        P(None, AXES, None),
        P(AXES, None),
        P(AXES, None),
        P(AXES, None),
        P(AXES),
        P(None, AXES),
        P(AXES),
        P(AXES, None),
    )
    out_specs = (P(AXES, None), P(None, AXES, None))
    return jax.shard_map(local, mesh=mesh, in_specs=in_specs, out_specs=out_specs, check_vma=False)
```

```python
import functools
import math

import jax
import jax.numpy as jnp
from jax import lax
from jax.experimental import pallas as pl
from jax.experimental.pallas import tpu as pltpu
from jax.sharding import PartitionSpec as P

KERNEL_NORM = 21.0 / (2.0 * math.pi)
AXES = ("gx", "gy")
LANES = 128
TILE = 256
ROWS = 64
CHUNKS = TILE // ROWS
TINY = 1e-30
F32 = jnp.float32
BF16 = jnp.bfloat16

ROW_NORM, ROW_ONE, ROW_H, ROW_MASS, ROW_G = 3, 4, 5, 6, 7

NN = (((1,), (0,)), ((), ()))
TN = (((0,), (0,)), ((), ()))
NT = (((1,), (1,)), ((), ()))


def mxu(a, b, dims):
    return lax.dot_general(a, b, dims, preferred_element_type=F32)


def pieces3(x):
    a = x.astype(BF16).astype(F32)
    r = x - a
    b = r.astype(BF16).astype(F32)
    c = r - b
    return a, b, c


def left_stack(x):
    a, b, c = pieces3(x)
    return jnp.concatenate([a, a, b, b, a, c], axis=0).astype(BF16)


def right_stack(x):
    a, b, c = pieces3(x)
    return jnp.concatenate([a, b, a, b, c, a], axis=0).astype(BF16)


def hi_lo_rows(x):
    hi = x.astype(BF16).astype(F32)
    return jnp.concatenate([hi, x - hi], axis=0).astype(BF16)


def twice(x):
    return jnp.concatenate([x, x], axis=1)


def row_fields(f_ref, i):
    block = f_ref[i >> 2, (i >> 1) & 1]
    return pltpu.roll(block, (i & 1) * ROWS, axis=1)[:, :ROWS]


def lane_fields(f_ref, j):
    return jnp.concatenate([f_ref[j, 0], f_ref[j, 1]], axis=1)


def distances(f_ref, pick, i, j):
    left = left_stack(row_fields(f_ref, i))
    lanes = lane_fields(f_ref, j)
    row = lax.broadcasted_iota(jnp.int32, (8, TILE), 0)
    norm = lanes[ROW_NORM : ROW_NORM + 1, :]
    right = jnp.where(row < 3, -32.0 * lanes, jnp.where(row == ROW_ONE, 16.0 * norm, jnp.where(row == ROW_NORM, 16.0, 0.0)))
    squared = mxu(left, right_stack(right), TN)
    return (squared,) if pick is None else (squared, mxu(left, pick, TN))


def lane_row(f_ref, j, which):
    return jnp.concatenate([f_ref[j, 0, which : which + 1, :], f_ref[j, 1, which : which + 1, :]], axis=1)


def fold_rows(x):
    total = x[0:8]
    for k in range(1, x.shape[0] // 8):
        total = total + x[8 * k : 8 * k + 8]
    return total


def add_lanes(out, j, values):
    out[j, 0] += values[:, :LANES]
    out[j, 1] += values[:, LANES:]


def add_rows(out, i, values):
    lane = lax.broadcasted_iota(jnp.int32, (8, LANES), 1)
    out[i >> 2, (i >> 1) & 1] += jnp.where((lane >> 6) == (i & 1), twice(values), 0.0)


def root(squared):
    squared = jnp.maximum(squared, TINY)
    return squared * lax.rsqrt(squared)


def density_self_values(parts, f_ref, i, j):
    squared, column = parts
    dist = root(squared)
    h = lane_row(f_ref, j, ROW_H)
    t = jnp.maximum(4.0 * h - dist, 0.0)
    t = t * t
    return fold_rows(t * t * (h + dist) * twice(column))


def density_pair_values(parts, f_ref, i, j):
    squared, column = parts
    dist = root(squared)
    h_row, m_row = twice(column[:, :LANES]), twice(column[:, LANES:])
    quarter = twice(0.25 * column[:, :LANES])
    h, m = lane_row(f_ref, j, ROW_H), lane_row(f_ref, j, ROW_MASS)
    t = jnp.maximum(h_row - dist, 0.0)
    t = t * t
    near = t * t * (quarter + dist) * m
    s = jnp.maximum(4.0 * h - dist, 0.0)
    s = s * s
    far = s * s * (h + dist) * m_row
    return (*hi_lo(near[:, :LANES] + near[:, LANES:]), fold_rows(far))


def density_pair_store(values, out, i, j):
    hi, lo, far = values
    add_lanes(out, j, far)
    one = (lax.broadcasted_iota(jnp.int32, (16, LANES), 0) == 0).astype(BF16)
    add_rows(out, i, (mxu(one, hi, NT) + mxu(one, lo, NT))[0:8])


def hi_lo(x):
    hi = x.astype(BF16)
    return hi, (x - hi.astype(F32)).astype(BF16)


def force_values(parts, f_ref, i, j):
    squared, column = parts
    dist = root(squared)
    h_row, g_row = twice(column[:, :LANES]), twice(column[:, LANES:])
    h, g = lane_row(f_ref, j, ROW_H), lane_row(f_ref, j, ROW_G)
    a = jnp.maximum(h_row - dist, 0.0)
    b = jnp.maximum(4.0 * h - dist, 0.0)
    return hi_lo(g_row * (a * a * a) + g * (b * b * b))


def moments(x):
    return hi_lo_rows(x * x[ROW_MASS : ROW_MASS + 1, :])


def force_self_values(parts, f_ref, i, j):
    b = jnp.maximum(4.0 * lane_row(f_ref, j, ROW_H) - root(parts[0]), 0.0)
    return hi_lo(b * b * b)


def force_self_store(values, f_ref, out, i, j):
    hi, lo = values
    g = lane_row(f_ref, j, ROW_G)
    rows = moments(row_fields(f_ref, i))
    add_lanes(out, j, g * fold_rows(mxu(rows, hi, NN) + mxu(rows, lo, NN)))
    lanes = lane_fields(f_ref, j)
    lanes = hi_lo_rows(lanes * (lanes[ROW_MASS : ROW_MASS + 1, :] * g))
    add_rows(out, i, fold_rows(mxu(lanes, hi, NT) + mxu(lanes, lo, NT)))


def force_store(values, f_ref, out, i, j):
    hi, lo = values
    rows = moments(row_fields(f_ref, i))
    add_lanes(out, j, fold_rows(mxu(rows, hi, NN) + mxu(rows, lo, NN)))
    lanes = moments(lane_fields(f_ref, j))
    add_rows(out, i, fold_rows(mxu(lanes, hi, NT) + mxu(lanes, lo, NT)))


def sweep(unroll, lead, lag, count, units, slots, stage_a, stage_b, stage_c):
    part_slots, value_slots = slots

    def unit(index):
        code = units[index]
        return code >> 16, code & 0xFFFF

    def save(refs, k, values):
        for ref, value in zip(refs, values):
            ref[k] = value

    def restore(refs, k):
        return tuple(ref[k] for ref in refs)

    for ref in value_slots:
        ref[...] = jnp.zeros_like(ref)
    for k in range(lead):
        save(part_slots, k, stage_a(*unit(k)))

    def body(step, carry):
        base = step * unroll
        ids = [unit(base + k) for k in range(unroll + lead)]
        behind = [unit(jnp.maximum(base - lag + k, 0)) for k in range(lag)]
        parts = {k: restore(part_slots, k) for k in range(lead)}
        values = {k - lag: restore(value_slots, k) for k in range(lag)}
        for k in range(unroll):
            parts[k + lead] = stage_a(*ids[k + lead])
            values[k] = stage_b(parts.pop(k), *ids[k])
            stage_c(values.pop(k - lag), *(behind[k] if k < lag else ids[k - lag]))
        for k in range(lead):
            save(part_slots, k, parts[unroll + k])
        for k in range(lag):
            save(value_slots, k, values[unroll - lag + k])
        return carry

    lax.fori_loop(0, count, body, 0)
    for k in range(lag):
        stage_c(restore(value_slots, k), *unit(jnp.maximum(count * unroll - lag + k, 0)))


HANDED = {"density_self": (2, 2), "density": (1, 2), "force_self": (2, 1), "force": (1, 2)}


def slot_shapes(kind):
    lead, lag = HANDED[kind]
    parts = [pltpu.VMEM((lead, ROWS, TILE), F32)]
    if kind == "density_self":
        parts.append(pltpu.VMEM((lead, ROWS, LANES), F32))
    elif kind != "force_self":
        parts.append(pltpu.VMEM((lead, ROWS, TILE), F32))
    if kind == "density_self":
        values = [pltpu.VMEM((lag, 8, TILE), F32)]
    elif kind == "density":
        values = [pltpu.VMEM((lag, ROWS, LANES), BF16)] * 2 + [pltpu.VMEM((lag, 8, TILE), F32)]
    else:
        values = [pltpu.VMEM((lag, ROWS, TILE), BF16)] * 2
    return (parts, values)


def sweep_kind(kind, unroll, count, units, f_ref, pick, out, slots):
    picked = {"density_self": pick[:, LANES:], "force_self": None}.get(kind, pick[...])
    middle = {
        "density_self": lambda p, i, j: (density_self_values(p, f_ref, i, j),),
        "density": lambda p, i, j: density_pair_values(p, f_ref, i, j),
        "force_self": lambda p, i, j: force_self_values(p, f_ref, i, j),
        "force": lambda p, i, j: force_values(p, f_ref, i, j),
    }
    last = {
        "density_self": lambda v, i, j: add_lanes(out, j, v[0]),
        "density": lambda v, i, j: density_pair_store(v, out, i, j),
        "force_self": lambda v, i, j: force_self_store(v, f_ref, out, i, j),
        "force": lambda v, i, j: force_store(v, f_ref, out, i, j),
    }
    sweep(
        unroll, *HANDED[kind], count[0], units, slots,
        lambda i, j: distances(f_ref, picked, i, j), middle[kind], last[kind],
    )


def density_scale(h):
    h2 = h * h
    h4 = h2 * h2
    return KERNEL_NORM / 256.0 / (h4 * h4)


def each_group(cells, body):
    def step(k, carry):
        for half in range(2):
            body(pl.multiple_of(k * 8, 8), half)
        return carry

    lax.fori_loop(0, cells // 8, step, 0)


def half_lanes(half):
    return slice(half * LANES, (half + 1) * LANES)


def prepare_kernel(counts, targets, pos, smooth, masses, fields, outgoing, alive):
    cells = smooth.shape[0]
    fields[cells] = jnp.zeros((2, 8, LANES), F32)
    sub = lax.broadcasted_iota(jnp.int32, (8, LANES), 0)
    lane = lax.broadcasted_iota(jnp.int32, (8, LANES), 1)

    def group(c, half):
        count = jnp.zeros((8, LANES), jnp.int32)
        for k in range(8):
            count = jnp.where(sub == k, counts[c + k], count)
        at = (pl.ds(c, 8), half_lanes(half))
        x, y, z = (pos[k, at[0], at[1]] - 0.5 for k in range(3))
        live = lane + half * LANES < count
        alive[at] = jnp.where(live, 1.0, 0.0)
        mass = jnp.where(live, masses[at], 0.0)
        rows = (x, y, z, x * x + y * y + z * z, jnp.ones_like(x), smooth[at], mass, count.astype(F32))
        for k in range(8):
            fields[pl.ds(c, 8), half, k, :] = rows[k]

    each_group(cells, group)

    def export(k, carry):
        for s in range(8):
            slot = k * 8 + s
            outgoing[slot] = fields[jnp.maximum(targets[slot], 0)]
        return carry

    lax.fori_loop(0, outgoing.shape[0] // 8, export, 0)


def load_fields(sources, f_ref, acc, sems):
    copies, first = [], 0
    for k, source in enumerate(sources):
        copies.append(pltpu.make_async_copy(source, f_ref.at[pl.ds(first, source.shape[0])], sems.at[k]))
        first += source.shape[0]
    for copy in copies:
        copy.start()
    acc[...] = jnp.zeros_like(acc)
    for copy in copies:
        copy.wait()


def density_inner_kernel(kind, unroll, count, units, f_ref, pick, out, acc, *slots):
    acc[...] = jnp.zeros_like(acc)
    sweep_kind(kind, unroll, count, units, f_ref, pick, acc, slots)

    def finish(c, half):
        out[pl.ds(c, 8), half_lanes(half)] = jnp.sum(acc[pl.ds(c, 8), half], axis=1)

    each_group(out.shape[0], finish)


def density_outer_kernel(unroll, count, units, own, ghosts, pick, own_out, ghost_out, f_ref, acc, sems, *slots):
    load_fields([own, ghosts], f_ref, acc, sems)
    sweep_kind("density", unroll, count, units, f_ref, pick, acc, slots)
    first = own.shape[0]

    def finish_own(c, half):
        own_out[pl.ds(c, 8), half_lanes(half)] = jnp.sum(acc[pl.ds(c, 8), half], axis=1)

    def finish_ghost(c, half):
        total = jnp.sum(acc[pl.ds(first + c, 8), half], axis=1)
        scale = density_scale(f_ref[pl.ds(first + c, 8), half, ROW_H, :])
        ghost_out[pl.ds(c, 8), 0, half_lanes(half)] = total * scale

    each_group(own_out.shape[0], finish_own)
    each_group(ghost_out.shape[0], finish_ghost)


def select(targets, cells):
    ids = lax.broadcasted_iota(jnp.int32, (cells, targets.shape[1]), 0)
    return (ids == targets[...]).astype(BF16)


def exact_dot(selector, values, dims):
    a, b, c = (x.astype(BF16) for x in pieces3(values))
    return mxu(selector, a, dims) + mxu(selector, b, dims) + mxu(selector, c, dims)


def factor_kernel(targets, self_rho, inner, outer, returned, alive, smooth, entropy, density, g_out, outgoing):
    cells = density.shape[0]
    selector = select(targets, cells)
    live = alive[...] > 0.0
    scale = density_scale(smooth[...])
    total = (self_rho[...] + inner[...] + outer[...]) * scale + exact_dot(selector, returned[:, 0, :], NN)
    rho = jnp.where(live, total, 0.0)
    density[...] = rho
    safe = jnp.where(live, rho, 1.0)
    g = jnp.where(live, entropy[...] * jnp.exp(jnp.log(safe) * (-1.0 / 3.0)) * (80.0 * scale), 0.0)
    g_out[...] = g
    outgoing[:, 0, :] = exact_dot(selector, g, TN)


def insert_g(f_ref, g, first, load):
    def body(c, half):
        f_ref[pl.ds(first + c, 8), half, ROW_G, :] = load(g, c, half)

    each_group(g.shape[0], body)


def natural(g, c, half):
    return g[pl.ds(c, 8), half_lanes(half)]


def by_slot(g, c, half):
    return g[pl.ds(c, 8), 0, half_lanes(half)]


def finish_force(f_ref, acc, out):
    def body(c, half):
        def row(ref, k):
            return ref[pl.ds(c, 8), half, k, :]

        live = row(f_ref, ROW_MASS) > 0.0
        total = row(acc, ROW_ONE)
        for k in range(3):
            out[k, pl.ds(c, 8), half_lanes(half)] = jnp.where(live, row(f_ref, k) * total - row(acc, k), 0.0)

    each_group(out.shape[1], body)


def force_inner_kernel(kind, unroll, count, units, own, own_g, pick, out, f_ref, acc, sems, *slots):
    load_fields([own], f_ref, acc, sems)
    insert_g(f_ref, own_g, 0, natural)
    sweep_kind(kind, unroll, count, units, f_ref, pick, acc, slots)
    finish_force(f_ref, acc, out)


def force_outer_kernel(unroll, count, units, own, ghosts, own_g, ghost_g, pick, own_out, ghost_out, f_ref, acc, sems, *slots):
    load_fields([own, ghosts], f_ref, acc, sems)
    first = own.shape[0]
    insert_g(f_ref, own_g, 0, natural)
    insert_g(f_ref, ghost_g, first, by_slot)
    sweep_kind("force", unroll, count, units, f_ref, pick, acc, slots)
    finish_force(f_ref, acc, own_out)

    def finish(k, carry):
        for s in range(4):
            for half in range(2):
                f, sums = f_ref[first + 4 * k + s, half], acc[first + 4 * k + s, half]
                live = f[ROW_MASS : ROW_MASS + 1, :] > 0.0
                ghost_out[4 * k + s, half] = jnp.where(live, f * sums[ROW_ONE : ROW_ONE + 1, :] - sums, 0.0)[0:4]
        return carry

    lax.fori_loop(0, ghost_out.shape[0] // 4, finish, 0)


def final_kernel(targets, self_acc, inner_acc, outer_acc, returned, acceleration):
    selector = select(targets, acceleration.shape[1])
    for half in range(2):
        lanes = half_lanes(half)
        for k in range(3):
            here = self_acc[k, :, lanes] + inner_acc[k, :, lanes] + outer_acc[k, :, lanes]
            acceleration[k, :, lanes] = here + exact_dot(selector, returned[:, half, k, :], NN)


SMEM = pl.BlockSpec(memory_space=pltpu.SMEM)
VMEM = pl.BlockSpec(memory_space=pltpu.VMEM)
ANY = pl.BlockSpec(memory_space=pl.ANY)


def launch(body, name, in_specs, shapes, args, scratch=(), flops=0, limit=40):
    return pl.pallas_call(
        body,
        out_shape=[jax.ShapeDtypeStruct(shape, F32) for shape in shapes],
        in_specs=in_specs,
        out_specs=[VMEM] * len(shapes),
        scratch_shapes=list(scratch),
        name=name,
        compiler_params=pltpu.CompilerParams(vmem_limit_bytes=limit * 1024 * 1024),
        cost_estimate=pl.CostEstimate(flops=flops, bytes_accessed=1 << 21, transcendentals=0),
    )(*args)


def pick_matrix(second):
    k = lax.broadcasted_iota(jnp.int32, (48, TILE), 0)
    lane = lax.broadcasted_iota(jnp.int32, (48, TILE), 1)
    group, row = k // 8, k % 8
    used = (group == 0) | (group == 2) | (group == 5)
    weight = jnp.where(lane < LANES, 4.0, 1.0)
    return jnp.where(used & (row == jnp.where(lane < LANES, ROW_H, second)), weight, 0.0).astype(BF16)


def compact(valid, code, spare, unroll):
    num = valid.shape[0]
    flags = valid.astype(jnp.int32)
    ids = jnp.arange(num, dtype=jnp.int32)
    rank = jnp.sum(jnp.where(ids[None, :] < ids[:, None], flags[None, :], 0), axis=1)
    total = jnp.sum(flags)
    hit = (rank[None, :] == ids[:, None]) & valid[None, :]
    listed = jnp.sum(jnp.where(hit, code[None, :], 0), axis=1)
    listed = jnp.where(ids < total, listed, spare)
    listed = jnp.concatenate([listed, jnp.full((LANES,), spare, listed.dtype)])
    return listed.astype(jnp.int32), ((total + unroll - 1) // unroll).reshape(1).astype(jnp.int32)


def look_up(table, ids):
    slots = jnp.arange(table.shape[0], dtype=jnp.int32)
    return jnp.sum(jnp.where(ids[:, None] == slots[None, :], table[None, :], 0), axis=1)


def pair_units(first, second, live, counts, spare, unroll):
    n_first, n_second = look_up(counts, first), look_up(counts, second)
    swap = n_second < n_first
    rows = jnp.where(swap, second, first)
    lanes = jnp.where(swap, first, second)
    chunks = (jnp.minimum(n_first, n_second) + ROWS - 1) // ROWS
    step = jnp.arange(CHUNKS, dtype=jnp.int32)
    valid = (step[None, :] < chunks[:, None]) & live[:, None]
    code = ((rows[:, None] * CHUNKS + step[None, :]) << 16) | lanes[:, None]
    return compact(valid.reshape(-1), code.reshape(-1), spare, unroll)


def trade(payload):
    peers = lax.axis_size(AXES)
    by_peer = payload.reshape(peers, -1, *payload.shape[2:-1], LANES)
    return lax.all_to_all(by_peer, AXES, split_axis=0, concat_axis=0, tiled=True).reshape(payload.shape)


def local(positions, smooth, masses, entropy, cell_counts, cell_pairs, pair_count, send_cells):
    cells, tile = smooth.shape
    num_pairs = cell_pairs.shape[1]
    slots = send_cells.shape[1]
    unroll = 40
    targets = send_cells[0]
    padded = (cells + 1, 2, 8, LANES)
    whole = (cells + 1 + slots, 2, 8, LANES)
    pick_m, pick_g = pick_matrix(ROW_MASS), pick_matrix(ROW_G)
    spare = ((cells * CHUNKS) << 16) | cells
    unit = ROWS * TILE * 2000
    both_sems = pltpu.SemaphoreType.DMA((2,))

    own, outgoing, alive = launch(
        prepare_kernel, "prepare", [SMEM, SMEM, VMEM, VMEM, VMEM], [padded, (slots, 2, 8, LANES), (cells, tile)],
        (cell_counts, targets, positions, smooth, masses),
    )
    ghosts = trade(outgoing)

    step = jnp.arange(CHUNKS, dtype=jnp.int32)
    ids = jnp.arange(cells, dtype=jnp.int32)
    self_valid = step[None, :] < ((cell_counts + ROWS - 1) // ROWS)[:, None]
    self_code = ((ids[:, None] * CHUNKS + step[None, :]) << 16) | ids[:, None]
    self_units, self_count = compact(self_valid.reshape(-1), self_code.reshape(-1), spare, unroll)
    live_pair = jnp.arange(num_pairs, dtype=jnp.int32) < pair_count[0]
    first, second = cell_pairs[0], cell_pairs[1]
    second = jnp.where(second < cells, second, second + 1)
    inner_units, inner_count = pair_units(first[slots:], second[slots:], live_pair[slots:], cell_counts, spare, unroll)

    def scratch(shape, kind):
        return [pltpu.VMEM(shape, F32), pltpu.VMEM(shape, F32), both_sems, *slot_shapes(kind)]

    (self_rho,) = launch(
        functools.partial(density_inner_kernel, "density_self", unroll), "density_self", [SMEM, SMEM, VMEM, VMEM],
        [(cells, tile)], (self_count, self_units, own, pick_m), [pltpu.VMEM(padded, F32), *slot_shapes("density_self")], 768 * unit,
    )
    ghosts, self_rho = lax.optimization_barrier((ghosts, self_rho))

    ghost_counts = jnp.max(ghosts[:, 0, ROW_G, :], axis=-1).astype(jnp.int32)
    all_counts = jnp.concatenate([cell_counts, jnp.zeros((1,), jnp.int32), ghost_counts])
    outer_units, outer_count = pair_units(first[:slots], second[:slots], live_pair[:slots], all_counts, spare, unroll)
    outer_rho, ghost_rho = launch(
        functools.partial(density_outer_kernel, unroll), "density_outer", [SMEM, SMEM, ANY, ANY, VMEM],
        [(cells, tile), (slots, 1, tile)], (outer_count, outer_units, own, ghosts, pick_m),
        scratch(whole, "density"), 640 * unit,
    )
    returned_rho = trade(ghost_rho)
    (inner_rho,) = launch(
        functools.partial(density_inner_kernel, "density", unroll), "density_inner", [SMEM, SMEM, VMEM, VMEM],
        [(cells, tile)], (inner_count, inner_units, own, pick_m), [pltpu.VMEM(padded, F32), *slot_shapes("density")], 320 * unit,
    )
    returned_rho, inner_rho = lax.optimization_barrier((returned_rho, inner_rho))

    density, own_g, outgoing_g = launch(
        factor_kernel, "factor", [VMEM] * 8, [(cells, tile), (cells, tile), (slots, 1, tile)],
        (send_cells, self_rho, inner_rho, outer_rho, returned_rho, alive, smooth, entropy),
    )
    ghost_g = trade(outgoing_g)
    (self_acc,) = launch(
        functools.partial(force_inner_kernel, "force_self", unroll), "force_self", [SMEM, SMEM, ANY, VMEM, VMEM],
        [(3, cells, tile)], (self_count, self_units, own, own_g, pick_g), scratch(padded, "force_self"), 768 * unit,
    )
    ghost_g, self_acc = lax.optimization_barrier((ghost_g, self_acc))

    outer_acc, ghost_acc = launch(
        functools.partial(force_outer_kernel, unroll), "force_outer", [SMEM, SMEM, ANY, ANY, VMEM, VMEM, VMEM],
        [(3, cells, tile), (slots, 2, 4, LANES)], (outer_count, outer_units, own, ghosts, own_g, ghost_g, pick_g),
        scratch(whole, "force"), 640 * unit,
    )
    returned_acc = trade(ghost_acc)
    (inner_acc,) = launch(
        functools.partial(force_inner_kernel, "force", unroll), "force_inner", [SMEM, SMEM, ANY, VMEM, VMEM],
        [(3, cells, tile)], (inner_count, inner_units, own, own_g, pick_g), scratch(padded, "force"), 320 * unit,
    )
    returned_acc, inner_acc = lax.optimization_barrier((returned_acc, inner_acc))

    (acceleration,) = launch(
        final_kernel, "final", [VMEM] * 5, [(3, cells, tile)],
        (send_cells, self_acc, inner_acc, outer_acc, returned_acc),
    )
    return (density, acceleration)


def solution(mesh):
    in_specs = (
        P(None, AXES, None),
        P(AXES, None),
        P(AXES, None),
        P(AXES, None),
        P(AXES),
        P(None, AXES),
        P(AXES),
        P(AXES, None),
    )
    out_specs = (P(AXES, None), P(None, AXES, None))
    return jax.shard_map(local, mesh=mesh, in_specs=in_specs, out_specs=out_specs, check_vma=False)
```
